32 devices in a mesh: seq: 16 (over z, y, x), head: 2 (over core).
Axes of the slice: x: 2, y: 2, z: 4, core: 2. Of those that a mesh axis runs over, the one named last changes fastest.
Arguments:
- queries: bfloat16 [8192, 32, 128], P('seq', 'head'), may hold values from -400 to 400
- key_vectors: bfloat16 [8192, 4, 128], P('seq', 'head'), may hold values from -400 to 400
- value_vectors: bfloat16 [8192, 4, 128], P('seq', 'head'), may hold values from -6 to 6
- query_map: bfloat16 [32, 128, 64], P('head'), may hold values from -0.5 to 0.5
- key_map: bfloat16 [32, 128, 64], P('head'), may hold values from -0.5 to 0.5
- window_param: float32 [32], P('head'), may hold values from 2 to 7
Outputs:
- attended: bfloat16 [32, 8192, 128], P(None, ('seq', 'head'))
The draws below stay inside these ranges and needn't reach their ends.
All inputs are finite; a program needn't handle non-finite values.
Results may differ from the reference program's by a relative error of at most 0.0013.
The reference program's roundings to bfloat16 on the way count: a program that leaves them out, or rounds other values in their place, can miss the bound.
Values may be sent and summed in bfloat16 or wider, within the bound.
No kernel may reach another device: no remote copies, remote signals or barrier semaphores. Data moves between devices by JAX's collectives and lax.ppermute only.
A program may use at most 320 MiB of HBM per device.

```python
import jax
import jax.numpy as jnp
from jax import lax

HEADS = 32
KV_HEADS = 4
HEAD_DIM = 128
FEAT = 64
WINDOW = 64
TOK_DEV = 512
TOKENS = 8192


def drawn_pair(base_key):
    pick_query, pick_key = jax.random.split(jax.random.fold_in(base_key, 7), 2)
    key_base = jax.random.normal(pick_key, (TOKENS, KV_HEADS, HEAD_DIM), jnp.float32)
    query_base = jax.random.normal(pick_query, (TOKENS, HEADS, HEAD_DIM), jnp.float32)
    return (query_base, key_base)


def draw_queries(key, part):
    return drawn_pair(key)[0].astype(jnp.bfloat16)


def draw_key_vectors(key, part):
    return drawn_pair(key)[1].astype(jnp.bfloat16)


def block_levels(stream_key, dims, shards, least, top_value):
    loudness = 1.0
    for axis_at, blocks in shards:
        heights = jax.random.uniform(jax.random.fold_in(jax.random.fold_in(stream_key, 6), axis_at), (blocks,), jnp.float32, least / len(shards), top_value / len(shards))
        loudness = loudness * jnp.repeat(jnp.exp(heights), dims[axis_at] // blocks).reshape((-1,) + (1,) * (len(dims) - 1 - axis_at))
    return loudness


def centred(stream_key, dims, width, limit, cuts=(), kind=jnp.bfloat16):
    loudness = block_levels(stream_key, dims, cuts, -0.22, 0.18) if cuts else 1.0
    entries = jax.random.normal(stream_key, dims, jnp.float32) * width * loudness
    return jnp.minimum(jnp.maximum(entries, -limit), limit).astype(kind)


def setup_inputs(seed: int = 0) -> dict:
    splits = jax.random.split(jax.random.key(seed), 7)
    queries = draw_queries(jax.random.fold_in(splits[6], 71), 0)
    key_vectors = draw_key_vectors(jax.random.fold_in(splits[6], 71), 0)
    value_vectors = centred(splits[2], (TOKENS, KV_HEADS, HEAD_DIM), 1.0, 6.0, ((0, 16), (1, 2)))
    query_map = centred(splits[3], (HEADS, HEAD_DIM, FEAT), HEAD_DIM ** -0.5, 0.5, ((0, 2),))
    key_map = centred(splits[4], (HEADS, HEAD_DIM, FEAT), HEAD_DIM ** -0.5, 0.5, ((0, 2),))
    window_param = jnp.clip(2.0 + 5.0 * jax.random.uniform(splits[5], (HEADS,), jnp.float32) ** block_levels(splits[5], (HEADS,), ((0, 2),), -0.2, 0.2), 2.0, 7.0)
    return dict(queries=queries, key_vectors=key_vectors, value_vectors=value_vectors, query_map=query_map, key_map=key_map, window_param=window_param)


def features(token_rows, weight):
    logits = jnp.dot(token_rows, weight, preferred_element_type=jnp.float32)
    both = jnp.concatenate([jax.nn.softmax(logits, axis=-1), jax.nn.softmax(-logits, axis=-1)], axis=-1)
    return both.astype(jnp.bfloat16)

def attend_head(query_rows, key_rows, value_rows, key_feat, weight_query, prior_state, prior_norm, mix_param, valid_keys):
    row_count = query_rows.shape[0]
    span_rows = key_rows.shape[0]
    window = span_rows - row_count
    scores = jnp.dot(query_rows, key_rows.T, preferred_element_type=jnp.float32) / jnp.sqrt(jnp.float32(query_rows.shape[1]))
    row_index = jnp.arange(row_count, dtype=jnp.int32)[:, None]
    col_index = jnp.arange(span_rows, dtype=jnp.int32)[None, :]
    distance = row_index + window - col_index
    in_window = (distance >= 0) & (distance < window) & valid_keys[None, :]
    in_linear = (distance >= window) & valid_keys[None, :]
    row_max = lax.optimization_barrier(jnp.max(jnp.where(in_window, scores, -1e+30), axis=-1, keepdims=True))
    window_prob = jnp.where(in_window, jnp.exp(scores - row_max), 0.0)
    window_sum = lax.optimization_barrier(jnp.sum(window_prob, axis=-1, keepdims=True))
    window_num = jnp.dot(window_prob.astype(jnp.bfloat16), value_rows, preferred_element_type=jnp.float32)
    query_feat = features(query_rows, weight_query)
    linear_weights = jnp.where(in_linear, jnp.dot(query_feat, key_feat.T, preferred_element_type=jnp.float32), 0.0)
    linear_sum = lax.optimization_barrier(jnp.sum(linear_weights, axis=-1, keepdims=True))
    linear_num = jnp.dot(linear_weights.astype(jnp.bfloat16), value_rows, preferred_element_type=jnp.float32)
    query_wide = query_feat.astype(jnp.float32)
    prior_num = jnp.dot(query_wide, prior_state, precision=lax.Precision.HIGHEST)
    prior_den = jnp.dot(query_wide, prior_norm[:, None], precision=lax.Precision.HIGHEST)
    mixing = jax.nn.sigmoid(mix_param)
    numer = mixing * window_num + (1.0 - mixing) * (linear_num + prior_num)
    denom = mixing * window_sum + (1.0 - mixing) * (linear_sum + prior_den)
    return (numer / denom).astype(jnp.bfloat16)

def reference(queries, key_vectors, value_vectors, query_map, key_map, window_param):
    row_count = TOK_DEV
    span_rows = WINDOW + row_count
    group_size = HEADS // KV_HEADS
    padding = jnp.zeros((WINDOW, KV_HEADS, HEAD_DIM), jnp.bfloat16)
    key_padded = jnp.concatenate([padding, key_vectors], axis=0)
    value_padded = jnp.concatenate([padding, value_vectors], axis=0)
    block_count = TOKENS // row_count

    def step(carry, block):
        state_all, norm_all = carry
        start = (block * row_count).astype(jnp.int32)
        key_block = lax.dynamic_slice_in_dim(key_padded, start, span_rows, 0)
        value_block = lax.dynamic_slice_in_dim(value_padded, start, span_rows, 0)
        query_block = lax.dynamic_slice_in_dim(queries, start, row_count, 0)
        valid_keys = start + jnp.arange(span_rows, dtype=jnp.int32) - WINDOW >= 0

        def one_head(head_index):
            group_index = head_index // group_size
            query_rows = lax.dynamic_index_in_dim(query_block, head_index, 1, keepdims=False)
            key_rows = lax.dynamic_index_in_dim(key_block, group_index, 1, keepdims=False)
            value_rows = lax.dynamic_index_in_dim(value_block, group_index, 1, keepdims=False)
            key_feat = features(key_rows, key_map[head_index])
            key_feat = jnp.where(valid_keys[:, None], key_feat, jnp.zeros_like(key_feat))
            result = attend_head(query_rows, key_rows, value_rows, key_feat, query_map[head_index], state_all[head_index], norm_all[head_index], window_param[head_index], valid_keys)
            add_state = jnp.dot(key_feat[:row_count].T, value_rows[:row_count], preferred_element_type=jnp.float32)
            add_norm = lax.optimization_barrier(jnp.sum(key_feat[:row_count].astype(jnp.float32), axis=0))
            return (result, add_state, add_norm)
        results, add_state, add_norm = lax.map(one_head, jnp.arange(HEADS, dtype=jnp.int32))
        return ((state_all + add_state, norm_all + add_norm), results)
    init = (jnp.zeros((HEADS, 2 * FEAT, HEAD_DIM), jnp.float32), jnp.zeros((HEADS, 2 * FEAT), jnp.float32))
    final, results = lax.scan(step, init, jnp.arange(block_count, dtype=jnp.int32))
    return results.transpose(1, 0, 2, 3).reshape(HEADS, TOKENS, HEAD_DIM)
```

```python
import functools

import jax
import jax.numpy as jnp
import numpy as np
from jax import lax
from jax.experimental import pallas as pl
from jax.experimental.pallas import tpu as pltpu
from jax.sharding import PartitionSpec as P

WINDOW = 64
PART = 4
BF = jnp.bfloat16
F32 = jnp.float32
BIG = 64 * 1024 * 1024


def mm(a, b, ca=1, cb=0):
    return lax.dot_general(a, b, (((ca,), (cb,)), ((), ())), preferred_element_type=F32)


def features_t(logits):
    top = jnp.max(logits, axis=0, keepdims=True)
    low = jnp.min(logits, axis=0, keepdims=True)
    up = jnp.exp(logits - top)
    down = jnp.exp(low - logits)
    up = up / jnp.sum(up, axis=0, keepdims=True)
    down = down / jnp.sum(down, axis=0, keepdims=True)
    return jnp.concatenate([up, down], axis=0).astype(BF)


def split_norm(state):
    width = state.shape[-1]
    norm = state[width : width + 1]
    high = norm.astype(BF).astype(F32)
    low = norm - high
    row = lax.broadcasted_iota(jnp.int32, (8, width), 0)
    tail = jnp.where(row == 0, high, jnp.where(row == 1, low, 0.0))
    return jnp.concatenate([state[:width], tail], axis=0).astype(BF)


def join_norm(piece):
    wide = piece.astype(F32)
    width = wide.shape[-1]
    norm = wide[width : width + 1] + wide[width + 1 : width + 2]
    row = lax.broadcasted_iota(jnp.int32, (8, width), 0)
    return jnp.concatenate([wide[:width], jnp.where(row == 0, norm, 0.0)], axis=0)


def values_with_one(values):
    row = lax.broadcasted_iota(jnp.int32, (8, values.shape[0]), 0)
    return jnp.concatenate([values.astype(F32).T, jnp.where(row == 0, 1.0, 0.0)], axis=0).astype(BF)


def state_kernel(per_part, group_size, idx_ref, k_ref, v_ref, w_ref, feat_ref, p0, p1, p2, p3, vt):
    step = pl.program_id(0)
    groups = k_ref.shape[0]

    @pl.when(step == 0)
    def _():
        for g in range(groups):
            vt[g] = values_with_one(v_ref[g])

    m = step // per_part
    head = lax.bitwise_xor(idx_ref[0], m) * per_part + step % per_part
    g = head // group_size
    feat = features_t(mm(w_ref[0], k_ref[g], 0, 1)).T
    feat_ref[0] = feat
    state = split_norm(mm(vt[g], feat))
    for k, out in enumerate((p0, p1, p2, p3)):

        @pl.when(m == k)
        def _(out=out):
            out[0] = state


def total_kernel(a, b, c, d, out):
    out[0] = split_norm(join_norm(a[0]) + join_norm(b[0]) + join_norm(c[0]) + join_norm(d[0]))


def prefix_kernel(zs, idx_ref, *refs):
    own, outs = refs[:PART], refs[PART + zs :]
    me = idx_ref[0]
    base = jnp.zeros(own[0].shape[1:], F32)
    for k in range(zs):
        base = base + join_norm(refs[PART + k][0])
    terms = [join_norm(r[0]) for r in own]
    for m in range(PART):
        total = base
        for k in range(PART):
            earlier = lax.bitwise_xor(me, k) < lax.bitwise_xor(me, m)
            total = total + jnp.where(earlier, terms[k], 0.0)
        outs[m][0] = split_norm(total)


def near_kernel(
    group_size, idx_ref, mix_ref, q_ref, k_ref, v_ref, hk_ref, hv_ref, feat_ref, wq_ref, wk_ref,
    num_ref, den_ref, qf_ref, tail_ref, q_wide, kx, vt, hv, fx,
):
    head = pl.program_id(0)
    rows, width = k_ref.shape[1:]
    scale = np.float32(np.log2(np.e) / np.sqrt(width))
    inner = head % group_size

    @pl.when(inner == 0)
    def _():
        q_wide[...] = q_ref[...].astype(F32).reshape(rows * group_size, width)
        kx[:WINDOW] = hk_ref[0]
        kx[WINDOW:] = k_ref[0]
        vt[...] = jnp.concatenate([hv_ref[0], v_ref[0]], axis=0).astype(F32).T.astype(BF)
        hv[...] = values_with_one(jnp.concatenate([hv_ref[0], hv_ref[0]], axis=0))

    present = idx_ref[1] > 0
    halo_logits = mm(wk_ref[0], kx[:128], 0, 1)
    halo_feat = features_t(halo_logits).T[:WINDOW]
    halo_feat = jnp.where(present, halo_feat.astype(F32), 0.0).astype(BF)
    fx[:WINDOW] = halo_feat
    fx[WINDOW:] = feat_ref[0]
    tail_ref[0] = mm(hv[:, :WINDOW], halo_feat)

    mix = mix_ref[head]
    rest = 1.0 - mix
    q = q_wide[pl.ds(inner, rows, stride=group_size), :].astype(BF)
    qf = features_t(mm(wq_ref[0], q, 0, 1))
    qf_ref[0] = qf

    block = 128
    span = block + WINDOW
    key = lax.broadcasted_iota(jnp.int32, (span, block), 0)
    row = lax.broadcasted_iota(jnp.int32, (span, block), 1)
    band = (key > row) & (key <= row + WINDOW)
    key_sq = lax.broadcasted_iota(jnp.int32, (block, block), 0)
    row_sq = lax.broadcasted_iota(jnp.int32, (block, block), 1)
    causal = key_sq <= row_sq
    for r in range(rows // block):
        at = r * block
        mask = (band & ((key >= WINDOW) | present)) if r == 0 else band
        s = mm(kx[at : at + span], q[at : at + block], 1, 1)
        s = jnp.where(mask, s, -1e30)
        p = jnp.exp2((s - jnp.max(s, axis=0, keepdims=True)) * scale)
        wsum = jnp.sum(p, axis=0, keepdims=True)
        wnum = mm(vt[:, at : at + span], p.astype(BF))
        a = mm(fx[: at + block], qf[:, at : at + block])
        last = jnp.where(causal, a[at:], 0.0)
        a = last if r == 0 else jnp.concatenate([a[:at], last], axis=0)
        lsum = jnp.sum(a, axis=0, keepdims=True)
        lnum = mm(vt[:, : at + block], a.astype(BF))
        num_ref[0, :, at : at + block] = mix * wnum + rest * lnum
        den_ref[0, :, at : at + block] = mix * wsum + rest * lsum


def final_kernel(idx_ref, mix_ref, num_ref, den_ref, qf_ref, tail_ref, state_ref, out_ref):
    rest = 1.0 - mix_ref[pl.program_id(0)]
    width = num_ref.shape[1]
    state = join_norm(state_ref[0, 0]) - tail_ref[0]
    high = state.astype(BF)
    low = (state - high.astype(F32)).astype(BF)
    both = mm(high, qf_ref[0]) + mm(low, qf_ref[0])
    numer = num_ref[0] + rest * both[:width]
    denom = den_ref[0] + rest * both[width : width + 1]
    out_ref[0] = (numer / denom).T.astype(BF)


def per_device(queries, key_vectors, value_vectors, query_map, key_map, window_param):
    rows, heads, width = queries.shape
    groups = key_vectors.shape[1]
    group_size = heads // groups
    feat = query_map.shape[2]
    per_part = heads // PART
    tall = width + 8
    devices = lax.axis_size("seq")
    zs = devices // PART
    position = lax.axis_index("seq")
    core = lax.axis_index("head")
    me = position % PART
    idx = jnp.stack([me, position, core, 1 - core]).astype(jnp.int32)
    mix = jax.nn.sigmoid(window_param)
    params = pltpu.CompilerParams(vmem_limit_bytes=BIG)
    smem = pl.BlockSpec(memory_space=pltpu.SMEM)

    def xor(x, m):
        return lax.ppermute(x, "seq", [(i, i ^ m) for i in range(devices)])

    def shift(x, by):
        return lax.ppermute(x, "seq", [(i, i + by) for i in range(devices - by)])

    keys = key_vectors.transpose(1, 0, 2)
    values = value_vectors.transpose(1, 0, 2)
    halo = shift(jnp.stack([keys[:, rows - WINDOW :], values[:, rows - WINDOW :]]), 1)

    def head_at(t, idx):
        return lax.bitwise_xor(idx[0], t // per_part) * per_part + t % per_part

    def piece_spec(m):
        return pl.BlockSpec((1, tall, width), lambda t, idx: (jnp.clip(t - m * per_part, 0, per_part - 1), 0, 0))

    whole = pl.BlockSpec((groups, rows, width), lambda t, idx: (0, 0, 0))
    own_feat, *pieces = pl.pallas_call(
        functools.partial(state_kernel, per_part, group_size),
        grid_spec=pltpu.PrefetchScalarGridSpec(
            num_scalar_prefetch=1,
            grid=(heads,),
            in_specs=[whole, whole, pl.BlockSpec((1, width, feat), lambda t, idx: (head_at(t, idx), 0, 0))],
            out_specs=[pl.BlockSpec((1, rows, width), lambda t, idx: (head_at(t, idx), 0, 0))]
            + [piece_spec(m) for m in range(PART)],
            scratch_shapes=[pltpu.VMEM((groups, tall, rows), BF)],
        ),
        out_shape=[jax.ShapeDtypeStruct((heads, rows, width), BF)]
        + [jax.ShapeDtypeStruct((per_part, tall, width), BF)] * PART,
        compiler_params=params,
        name="states",
    )(idx, keys, values, key_map)

    pieces = [pieces[0]] + [xor(pieces[m], m) for m in range(1, PART)]
    one = pl.BlockSpec((1, tall, width), lambda t, *_: (t, 0, 0))
    piece_shape = jax.ShapeDtypeStruct((per_part, tall, width), BF)
    total = pl.pallas_call(
        total_kernel, grid=(per_part,), in_specs=[one] * PART, out_specs=one, out_shape=piece_shape, name="totals"
    )(*pieces)
    if zs <= 4:
        earlier = [shift(total, PART * k) for k in range(1, zs)]
    else:
        columns = [[z * PART + k for z in range(zs)] for k in range(PART)]
        gathered = lax.all_gather(total, "seq", axis_index_groups=columns)
        earlier = [jnp.where(k < position // PART, gathered[k], jnp.zeros_like(total)) for k in range(zs - 1)]
    prefixes = pl.pallas_call(
        functools.partial(prefix_kernel, len(earlier)),
        grid_spec=pltpu.PrefetchScalarGridSpec(
            num_scalar_prefetch=1, grid=(per_part,), in_specs=[one] * (PART + len(earlier)), out_specs=[one] * PART
        ),
        out_shape=[piece_shape] * PART,
        name="prefixes",
    )(idx, *pieces, *earlier)
    prior = jnp.stack([prefixes[0]] + [xor(prefixes[m], m) for m in range(1, PART)])

    def per_head(*dims):
        return pl.BlockSpec((1,) + dims, lambda h, *_: (h,) + (0,) * len(dims))

    def per_group(*dims):
        return pl.BlockSpec((1,) + dims, lambda h, *_: (h // group_size,) + (0,) * len(dims))

    num, den, qf, tail = pl.pallas_call(
        functools.partial(near_kernel, group_size),
        grid_spec=pltpu.PrefetchScalarGridSpec(
            num_scalar_prefetch=1,
            grid=(heads,),
            in_specs=[
                smem,
                pl.BlockSpec((rows, group_size, width), lambda h, *_: (0, h // group_size, 0)),
                per_group(rows, width),
                per_group(rows, width),
                per_group(WINDOW, width),
                per_group(WINDOW, width),
                per_head(rows, width),
                per_head(width, feat),
                per_head(width, feat),
            ],
            out_specs=[
                per_head(width, rows),
                per_head(1, rows),
                per_head(2 * feat, rows),
                per_head(tall, width),
            ],
            scratch_shapes=[
                pltpu.VMEM((rows * group_size, width), F32),
                pltpu.VMEM((WINDOW + rows, width), BF),
                pltpu.VMEM((width, WINDOW + rows), BF),
                pltpu.VMEM((tall, 2 * WINDOW), BF),
                pltpu.VMEM((WINDOW + rows, 2 * feat), BF),
            ],
        ),
        out_shape=[
            jax.ShapeDtypeStruct((heads, width, rows), F32),
            jax.ShapeDtypeStruct((heads, 1, rows), F32),
            jax.ShapeDtypeStruct((heads, 2 * feat, rows), BF),
            jax.ShapeDtypeStruct((heads, tall, width), F32),
        ],
        compiler_params=params,
        cost_estimate=pl.CostEstimate(flops=6 * 10**9, bytes_accessed=14 * 10**6, transcendentals=4 * 10**6),
        name="near",
    )(idx, mix, queries, keys, values, halo[0], halo[1], own_feat, query_map, key_map)

    half = rows // 2

    def finish(name, which, out_heads, out_map):
        def half_of(dims):
            return pl.BlockSpec((1, dims, half), lambda h, idx: (h, 0, idx[which]))

        return pl.pallas_call(
            final_kernel,
            grid_spec=pltpu.PrefetchScalarGridSpec(
                num_scalar_prefetch=1,
                grid=(heads,),
                in_specs=[
                    smem,
                    half_of(width),
                    half_of(1),
                    half_of(2 * feat),
                    per_head(tall, width),
                    pl.BlockSpec(
                        (1, 1, tall, width),
                        lambda h, idx: (lax.bitwise_xor(idx[0], h // per_part), h % per_part, 0, 0),
                    ),
                ],
                out_specs=pl.BlockSpec((1, half, width), out_map),
            ),
            out_shape=jax.ShapeDtypeStruct((out_heads, half, width), BF),
            compiler_params=params,
            cost_estimate=pl.CostEstimate(flops=10**9, bytes_accessed=5 * 10**6, transcendentals=0),
            name=name,
        )(idx, mix, num, den, qf, tail, prior)

    theirs = finish("final_sent", 3, heads, lambda h, idx: (h, 0, 0))
    got = lax.ppermute(theirs, "head", [(0, 1), (1, 0)])
    out = finish("final_kept", 2, 2 * heads, lambda h, idx: (h + heads * idx[2], 0, 0))
    return lax.dynamic_update_slice(out, got, (heads * (1 - core), 0, 0))


def solution(mesh):
    in_specs = (
        P("seq", "head", None),
        P("seq", "head", None),
        P("seq", "head", None),
        P("head", None, None),
        P("head", None, None),
        P("head"),
    )
    out_specs = P(None, ("seq", "head"), None)
    return jax.shard_map(
        per_device, mesh=mesh, in_specs=in_specs, out_specs=out_specs, check_vma=False
    )
```

```python
import functools

import jax
import jax.numpy as jnp
import numpy as np
from jax import lax
from jax.experimental import pallas as pl
from jax.experimental.pallas import tpu as pltpu
from jax.sharding import PartitionSpec as P

WINDOW = 64
PART = 4
BF = jnp.bfloat16
F32 = jnp.float32
LIMIT = 64 * 1024 * 1024
STEP = 2
SPLIT = (4, 12)


def mm(a, b, ca=1, cb=0):
    return lax.dot_general(a, b, (((ca,), (cb,)), ((), ())), preferred_element_type=F32)


def features_t(logits):
    top = jnp.max(logits, axis=0, keepdims=True)
    low = jnp.min(logits, axis=0, keepdims=True)
    up = jnp.exp(logits - top)
    down = jnp.exp(low - logits)
    up = up / jnp.sum(up, axis=0, keepdims=True)
    down = down / jnp.sum(down, axis=0, keepdims=True)
    return jnp.concatenate([up, down], axis=0).astype(BF)


def split_norm(state):
    width = state.shape[-1]
    norm = state[width : width + 1]
    high = norm.astype(BF).astype(F32)
    low = norm - high
    row = lax.broadcasted_iota(jnp.int32, (8, width), 0)
    tail = jnp.where(row == 0, high, jnp.where(row == 1, low, 0.0))
    return jnp.concatenate([state[:width], tail], axis=0).astype(BF)


def join_norm(piece):
    wide = piece.astype(F32)
    width = wide.shape[-1]
    norm = wide[width : width + 1] + wide[width + 1 : width + 2]
    row = lax.broadcasted_iota(jnp.int32, (8, width), 0)
    return jnp.concatenate([wide[:width], jnp.where(row == 0, norm, 0.0)], axis=0)


def values_with_one(values):
    row = lax.broadcasted_iota(jnp.int32, (8, values.shape[0]), 0)
    return jnp.concatenate([values.astype(F32).T, jnp.where(row == 0, 1.0, 0.0)], axis=0).astype(BF)


def state_kernel(per_part, group_size, idx_ref, k_ref, v_ref, w_ref, feat_ref, kg_ref, vg_ref, p0, p1, p2, p3, vt):
    m = pl.program_id(0)
    rows, groups, width = k_ref.shape

    @pl.when(m == 0)
    def _():
        wide_k = k_ref[...].astype(F32)
        wide_v = v_ref[...].astype(F32)
        for g in range(groups):
            kg_ref[g] = wide_k[:, g].astype(BF)
            values = wide_v[:, g].astype(BF)
            vg_ref[g] = values
            vt[g] = values_with_one(values)

    g = lax.bitwise_xor(idx_ref[0], m) * per_part // group_size
    logits = mm(w_ref[...].reshape(-1, width), kg_ref[g], 1, 1)
    states = []
    for e in range(per_part):
        f = logits.shape[0] // per_part
        feat = features_t(logits[e * f : (e + 1) * f]).T
        feat_ref[e] = feat
        states.append(split_norm(mm(vt[g], feat)))
    for k, out in enumerate((p0, p1, p2, p3)):

        @pl.when(m == k)
        def _(out=out):
            for e in range(per_part):
                out[e] = states[e]


def total_kernel(a, b, c, d, _, out):
    for e in range(out.shape[0]):
        out[e] = split_norm(join_norm(a[e]) + join_norm(b[e]) + join_norm(c[e]) + join_norm(d[e]))


def prefix_kernel(zs, idx_ref, *refs):
    own, outs = refs[:PART], refs[PART + zs + 1 :]
    me = idx_ref[0]
    for e in range(outs[0].shape[0]):
        base = jnp.zeros(own[0].shape[1:], F32)
        for k in range(zs):
            base = base + join_norm(refs[PART + k][e])
        terms = [join_norm(r[e]) for r in own]
        for m in range(PART):
            total = base
            for k in range(PART):
                earlier = lax.bitwise_xor(me, k) < lax.bitwise_xor(me, m)
                total = total + jnp.where(earlier, terms[k], 0.0)
            outs[m][e] = split_norm(total)


def near_kernel(
    group_size, first, idx_ref, share_ref, q_ref, k_ref, v_ref, hk_ref, hv_ref, feat_ref, wq_ref, wk_ref, *refs
):
    num_ref, den_ref, qf_ref, tail_ref, q_wide, kx, vt, hv, fx = refs[-9:]
    step = pl.program_id(0)
    count = feat_ref.shape[0]
    head = first + step * count
    rows, width = k_ref.shape[1:]
    scale = np.float32(np.log2(np.e) / np.sqrt(width))

    @pl.when((step == 0) | (head % group_size == 0))
    def _():
        q_wide[...] = q_ref[...].astype(F32).reshape(rows * group_size, width)
        kx[:WINDOW] = hk_ref[0]
        kx[WINDOW:] = k_ref[0]
        vt[...] = jnp.concatenate([hv_ref[0], v_ref[0]], axis=0).astype(F32).T.astype(BF)
        hv[...] = values_with_one(jnp.concatenate([hv_ref[0], hv_ref[0]], axis=0))

    present = idx_ref[1] > 0
    block = 128
    span = block + WINDOW
    key = lax.broadcasted_iota(jnp.int32, (span, block), 0)
    row = lax.broadcasted_iota(jnp.int32, (span, block), 1)
    band = (key > row) & (key <= row + WINDOW)
    key_sq = lax.broadcasted_iota(jnp.int32, (block, block), 0)
    row_sq = lax.broadcasted_iota(jnp.int32, (block, block), 1)
    causal = key_sq <= row_sq
    for e in range(count):
        halo_feat = features_t(mm(wk_ref[e], kx[:128], 1, 1)).T[:WINDOW]
        halo_feat = jnp.where(present, halo_feat.astype(F32), 0.0).astype(BF)
        fx[e, :WINDOW] = halo_feat
        fx[e, WINDOW:] = feat_ref[e]
        tail_ref[e] = mm(hv[:, :WINDOW], halo_feat)

        mix = jax.nn.sigmoid(jnp.full((1, block), share_ref[head + e], F32))
        rest = 1.0 - mix
        q = q_wide[pl.ds(head % group_size + e, rows, stride=group_size), :].astype(BF)
        qf = features_t(mm(wq_ref[e], q, 1, 1))
        qf_ref[e] = qf
        for r in range(rows // block):
            at = r * block
            mask = (band & ((key >= WINDOW) | present)) if r == 0 else band
            s = mm(kx[at : at + span], q[at : at + block], 1, 1)
            s = jnp.where(mask, s, -1e30)
            p = jnp.exp2((s - jnp.max(s, axis=0, keepdims=True)) * scale)
            wsum = jnp.sum(p, axis=0, keepdims=True)
            wnum = mm(vt[:, at : at + span], p.astype(BF))
            a = mm(fx[e, : at + block], qf[:, at : at + block])
            last = jnp.where(causal, a[at:], 0.0)
            a = last if r == 0 else jnp.concatenate([a[:at], last], axis=0)
            lsum = jnp.sum(a, axis=0, keepdims=True)
            lnum = mm(vt[:, : at + block], a.astype(BF))
            num_ref[e, :, at : at + block] = mix * wnum + rest * lnum
            den_ref[e, :, at : at + block] = mix * wsum + rest * lsum


def final_kernel(idx_ref, share_ref, num_ref, den_ref, qf_ref, tail_ref, state_ref, out_ref):
    count, width, rows = num_ref.shape
    for e in range(count):
        share = share_ref[pl.program_id(0) * count + e]
        rest = 1.0 - jax.nn.sigmoid(jnp.full((1, rows), share, F32))
        state = join_norm(state_ref[0, e]) - tail_ref[e]
        high = state.astype(BF)
        low = (state - high.astype(F32)).astype(BF)
        both = mm(high, qf_ref[e]) + mm(low, qf_ref[e])
        numer = num_ref[e] + rest * both[:width]
        denom = den_ref[e] + rest * both[width : width + 1]
        out_ref[e] = (numer * (1.0 / denom)).astype(BF).T


def per_device(queries, key_vectors, value_vectors, query_map, key_map, window_param):
    rows, heads, width = queries.shape
    groups = key_vectors.shape[1]
    group_size = heads // groups
    feat = query_map.shape[2]
    per_part = heads // PART
    tall = width + 8
    devices = lax.axis_size("seq")
    zs = devices // PART
    position = lax.axis_index("seq")
    core = lax.axis_index("head")
    me = position % PART
    idx = jnp.stack([me, position, core, 1 - core]).astype(jnp.int32)
    params = pltpu.CompilerParams(vmem_limit_bytes=LIMIT)
    smem = pl.BlockSpec(memory_space=pltpu.SMEM)
    anywhere = pl.BlockSpec(memory_space=pl.ANY)
    query_map = query_map.transpose(0, 2, 1)
    key_map = key_map.transpose(0, 2, 1)

    def xor(x, m):
        return lax.ppermute(x, "seq", [(i, i ^ m) for i in range(devices)])

    def shift(x, by):
        return lax.ppermute(x, "seq", [(i, i + by) for i in range(devices - by)])

    halo = shift(jnp.stack([key_vectors[rows - WINDOW :], value_vectors[rows - WINDOW :]]).transpose(0, 2, 1, 3), 1)

    def part_of(m, idx):
        return lax.bitwise_xor(idx[0], m)

    raw = pl.BlockSpec((rows, groups, width), lambda m, idx: (0, 0, 0))
    whole = pl.BlockSpec((groups, rows, width), lambda m, idx: (0, 0, 0))
    piece = pl.BlockSpec((per_part, tall, width), lambda m, idx: (0, 0, 0))
    piece_shape = jax.ShapeDtypeStruct((per_part, tall, width), BF)
    own_feat, keys, values, *pieces = pl.pallas_call(
        functools.partial(state_kernel, per_part, group_size),
        grid_spec=pltpu.PrefetchScalarGridSpec(
            num_scalar_prefetch=1,
            grid=(PART,),
            in_specs=[raw, raw, pl.BlockSpec((per_part, feat, width), lambda m, idx: (part_of(m, idx), 0, 0))],
            out_specs=[pl.BlockSpec((per_part, rows, width), lambda m, idx: (part_of(m, idx), 0, 0)), whole, whole]
            + [piece] * PART,
            scratch_shapes=[pltpu.VMEM((groups, tall, rows), BF)],
        ),
        out_shape=[jax.ShapeDtypeStruct((heads, rows, width), BF)]
        + [jax.ShapeDtypeStruct((groups, rows, width), BF)] * 2
        + [piece_shape] * PART,
        compiler_params=params,
        name="states",
    )(idx, key_vectors, value_vectors, key_map)

    def per_group(first, *dims):
        return pl.BlockSpec((1,) + dims, lambda h, *_: ((first + h * STEP) // group_size,) + (0,) * len(dims))

    near_shapes = [
        jax.ShapeDtypeStruct((heads, width, rows), F32),
        jax.ShapeDtypeStruct((heads, 1, rows), F32),
        jax.ShapeDtypeStruct((heads, 2 * feat, rows), BF),
        jax.ShapeDtypeStruct((heads, tall, width), F32),
    ]

    def near(first, count, before, after):
        def per_head(*dims):
            return pl.BlockSpec((STEP,) + dims, lambda h, *_: (first // STEP + h,) + (0,) * len(dims))

        return pl.pallas_call(
            functools.partial(near_kernel, group_size, first),
            grid_spec=pltpu.PrefetchScalarGridSpec(
                num_scalar_prefetch=1,
                grid=(count // STEP,),
                in_specs=[
                    smem,
                    pl.BlockSpec((rows, group_size, width), lambda h, *_: (0, (first + h * STEP) // group_size, 0)),
                    per_group(first, rows, width),
                    per_group(first, rows, width),
                    per_group(first, WINDOW, width),
                    per_group(first, WINDOW, width),
                    per_head(rows, width),
                    per_head(feat, width),
                    per_head(feat, width),
                ]
                + [anywhere] * (len(before) + len(after)),
                out_specs=[per_head(width, rows), per_head(1, rows), per_head(2 * feat, rows), per_head(tall, width)],
                scratch_shapes=[
                    pltpu.VMEM((rows * group_size, width), F32),
                    pltpu.VMEM((WINDOW + rows, width), BF),
                    pltpu.VMEM((width, WINDOW + rows), BF),
                    pltpu.VMEM((tall, 2 * WINDOW), BF),
                    pltpu.VMEM((STEP, WINDOW + rows, 2 * feat), BF),
                ],
            ),
            out_shape=near_shapes,
            input_output_aliases={10 + k: k for k in range(len(before))},
            compiler_params=params,
            cost_estimate=pl.CostEstimate(
                flops=count * 4 * 10**8, bytes_accessed=count * 10**6, transcendentals=count * 3 * 10**5
            ),
            name="near_%d" % first,
        )(idx, window_param, queries, keys, values, halo[0], halo[1], own_feat, query_map, key_map, *before, *after)

    pieces = [pieces[0]] + [xor(pieces[m], m) for m in range(1, PART)]
    held = near(0, SPLIT[0], [], [])
    vmem = pl.BlockSpec(memory_space=pltpu.VMEM)
    total = pl.pallas_call(
        total_kernel, in_specs=[vmem] * PART + [anywhere], out_specs=vmem, out_shape=piece_shape, name="totals"
    )(*pieces, held[1])
    if zs <= 4:
        earlier = [shift(total, PART * k) for k in range(1, zs)]
    else:
        columns = [[z * PART + k for z in range(zs)] for k in range(PART)]
        gathered = lax.all_gather(total, "seq", axis_index_groups=columns)
        below = jnp.arange(zs) < position // PART
        summed = jnp.sum(jnp.where(below[:, None, None, None], gathered.astype(F32), 0.0), axis=0)
        high = summed.astype(BF)
        earlier = [high, (summed - high.astype(F32)).astype(BF)]
    held = near(SPLIT[0], SPLIT[1] - SPLIT[0], held, [total])
    prefixes = pl.pallas_call(
        functools.partial(prefix_kernel, len(earlier)),
        in_specs=[smem] + [vmem] * (PART + len(earlier)) + [anywhere],
        out_specs=[vmem] * PART,
        out_shape=[piece_shape] * PART,
        name="prefixes",
    )(idx, *pieces, *earlier, held[1])
    prior = jnp.stack([prefixes[0]] + [xor(prefixes[m], m) for m in range(1, PART)])
    num, den, qf, tail = near(SPLIT[1], heads - SPLIT[1], held, [prefixes[0]])

    half = rows // 2

    def finish(name, which, out_heads, out_at):
        def half_of(dims):
            return pl.BlockSpec((per_part, dims, half), lambda h, idx: (h, 0, idx[which]))

        return pl.pallas_call(
            final_kernel,
            grid_spec=pltpu.PrefetchScalarGridSpec(
                num_scalar_prefetch=1,
                grid=(PART,),
                in_specs=[
                    smem,
                    half_of(width),
                    half_of(1),
                    half_of(2 * feat),
                    pl.BlockSpec((per_part, tall, width), lambda h, *_: (h, 0, 0)),
                    pl.BlockSpec((1, per_part, tall, width), lambda h, idx: (part_of(h, idx), 0, 0, 0)),
                ],
                out_specs=pl.BlockSpec((per_part, half, width), lambda h, idx: (h + out_at(idx), 0, 0)),
            ),
            out_shape=jax.ShapeDtypeStruct((out_heads, half, width), BF),
            compiler_params=params,
            cost_estimate=pl.CostEstimate(flops=10**9, bytes_accessed=5 * 10**6, transcendentals=0),
            name=name,
        )(idx, window_param, num, den, qf, tail, prior)

    theirs = finish("final_sent", 3, heads, lambda idx: 0)
    got = lax.ppermute(theirs, "head", [(0, 1), (1, 0)])
    out = finish("final_kept", 2, 2 * heads, lambda idx: PART * idx[2])
    return lax.dynamic_update_slice(out, got, (heads * (1 - core), 0, 0))


def solution(mesh):
    in_specs = (
        P("seq", "head", None),
        P("seq", "head", None),
        P("seq", "head", None),
        P("head", None, None),
        P("head", None, None),
        P("head"),
    )
    out_specs = P(None, ("seq", "head"), None)
    return jax.shard_map(
        per_device, mesh=mesh, in_specs=in_specs, out_specs=out_specs, check_vma=False
    )
```

```python
import functools

import jax
import jax.numpy as jnp
import numpy as np
from jax import lax
from jax.experimental import pallas as pl
from jax.experimental.pallas import tpu as pltpu
from jax.sharding import PartitionSpec as P

WINDOW = 64
PART = 4
BF = jnp.bfloat16
F32 = jnp.float32
LIMIT = 16 * 1024 * 1024
STEP = 2
SPLIT = (4, 12)


def mm(a, b, ca=1, cb=0):
    return lax.dot_general(a, b, (((ca,), (cb,)), ((), ())), preferred_element_type=F32)


def features_t(logits):
    top = jnp.max(logits, axis=0, keepdims=True)
    low = jnp.min(logits, axis=0, keepdims=True)
    up = jnp.exp(logits - top)
    down = jnp.exp(low - logits)
    up = up * (1.0 / jnp.sum(up, axis=0, keepdims=True))
    down = down * (1.0 / jnp.sum(down, axis=0, keepdims=True))
    return jnp.concatenate([up, down], axis=0).astype(BF)


def split_norm(state):
    width = state.shape[-1]
    norm = state[width : width + 1]
    high = norm.astype(BF).astype(F32)
    low = norm - high
    row = lax.broadcasted_iota(jnp.int32, (8, width), 0)
    tail = jnp.where(row == 0, high, jnp.where(row == 1, low, 0.0))
    return jnp.concatenate([state[:width], tail], axis=0).astype(BF)


def join_norm(piece):
    wide = piece.astype(F32)
    width = wide.shape[-1]
    norm = wide[width : width + 1] + wide[width + 1 : width + 2]
    row = lax.broadcasted_iota(jnp.int32, (8, width), 0)
    return jnp.concatenate([wide[:width], jnp.where(row == 0, norm, 0.0)], axis=0)


def values_with_one(values):
    row = lax.broadcasted_iota(jnp.int32, (8, values.shape[0]), 0)
    return jnp.concatenate([values.T, jnp.where(row == 0, 1.0, 0.0).astype(BF)], axis=0)


def state_kernel(per_part, group_size, idx_ref, k_ref, v_ref, w_ref, feat_ref, kg_ref, vg_ref, p0, p1, p2, p3, vt):
    rows, groups, width = k_ref.shape
    wide_k = k_ref[...].astype(F32)
    wide_v = v_ref[...].astype(F32)
    for g in range(groups):
        kg_ref[g] = wide_k[:, g].astype(BF)
        values = wide_v[:, g].astype(BF)
        vg_ref[g] = values
        vt[g] = values_with_one(values)
    for m, out in enumerate((p0, p1, p2, p3)):
        head = lax.bitwise_xor(idx_ref[0], m) * per_part
        g = head // group_size
        logits = mm(w_ref[pl.ds(head, per_part)].reshape(-1, width), kg_ref[g], 1, 1)
        for e in range(per_part):
            f = logits.shape[0] // per_part
            feat = features_t(logits[e * f : (e + 1) * f]).T
            feat_ref[head + e] = feat
            out[e] = split_norm(mm(vt[g], feat))


def total_kernel(a, b, c, d, _, out):
    for e in range(out.shape[0]):
        out[e] = split_norm(join_norm(a[e]) + join_norm(b[e]) + join_norm(c[e]) + join_norm(d[e]))


def prefix_kernel(zs, idx_ref, *refs):
    own, outs = refs[:PART], refs[PART + zs + 1 :]
    me = idx_ref[0]
    for e in range(outs[0].shape[0]):
        base = jnp.zeros(own[0].shape[1:], F32)
        for k in range(zs):
            base = base + join_norm(refs[PART + k][e])
        terms = [join_norm(r[e]) for r in own]
        for m in range(PART):
            total = base
            for k in range(PART):
                earlier = lax.bitwise_xor(me, k) < lax.bitwise_xor(me, m)
                total = total + jnp.where(earlier, terms[k], 0.0)
            outs[m][e] = split_norm(total)


def prepare_kernel(group_size, q_ref, k_ref, v_ref, halo_ref, q_wide, kx, vt):
    rows, _, width = q_ref.shape
    wide = halo_ref[...].astype(F32)
    for g in range(k_ref.shape[0]):
        q = q_ref[:, g * group_size : (g + 1) * group_size].astype(F32)
        q_wide[g] = q.reshape(rows * group_size, width)
        kx[g, :WINDOW] = wide[0, :, g].astype(BF)
        kx[g, WINDOW:] = k_ref[g]
        vt[g] = jnp.concatenate([wide[1, :, g].astype(BF), v_ref[g]], axis=0).T


def near_kernel(group_size, first, count, idx_ref, share_ref, q_wide, kx_ref, vt_ref, feat_ref, wq_ref, wk_ref, *refs):
    num_ref, den_ref, qf_ref, fx = refs[-4:]
    out = pl.program_id(0) * count
    head = first + out
    g = head // group_size
    rows, width = feat_ref.shape[1:]
    scale = np.float32(np.log2(np.e) / np.sqrt(width))
    kx, vt = kx_ref.at[g], vt_ref.at[g]
    present = idx_ref[1] > 0
    block = 128
    span = block + WINDOW
    key = lax.broadcasted_iota(jnp.int32, (span, 2 * block), 0)
    row = lax.broadcasted_iota(jnp.int32, (span, 2 * block), 1) % block
    band = (key > row) & (key <= row + WINDOW)
    wide = 2 * block
    causal = lax.broadcasted_iota(jnp.int32, (wide, wide), 0) <= lax.broadcasted_iota(jnp.int32, (wide, wide), 1)
    halo_logits = mm(wk_ref[pl.ds(head, count)].reshape(-1, width), kx[:128], 1, 1)
    feat = halo_logits.shape[0] // count
    for pair in range(0, count, 2):
        qs, mixes, rests, lnums, lsums = [], [], [], [], []
        for e in (pair, pair + 1):
            halo_feat = features_t(halo_logits[e * feat : (e + 1) * feat]).T[:WINDOW]
            fx[e, :WINDOW] = jnp.where(present, halo_feat.astype(F32), 0.0).astype(BF)
            fx[e, WINDOW:] = feat_ref[head + e]
            mixes.append(jax.nn.sigmoid(jnp.full((1, block), share_ref[head + e], F32)))
            rests.append(1.0 - mixes[-1])
            q = q_wide[g, pl.ds(head % group_size + e, rows, stride=group_size), :].astype(BF)
            qs.append(q)
            qf = features_t(mm(wq_ref[head + e], q, 1, 1))
            qf_ref[out + e] = qf
            for r in range(rows // wide):
                at = r * wide
                lnum = None
                lsum = None
                for kc in range(r + 1):
                    a = mm(fx[e, kc * wide : kc * wide + wide], qf[:, at : at + wide])
                    if kc == r:
                        last = jnp.where(causal, a, 0.0)
                    else:
                        last = a
                    if kc == 0:
                        halo = a[:WINDOW]
                        kept = halo.astype(BF).astype(F32)
                        body = last[WINDOW:]
                        part = jnp.sum(body, axis=0, keepdims=True)
                        if r == 0:
                            inside = causal[:WINDOW]
                            kept = jnp.where(inside, kept, 0.0)
                            part = part - jnp.sum(jnp.where(inside, 0.0, halo), axis=0, keepdims=True)
                        w = jnp.concatenate([(kept - halo).astype(BF), body.astype(BF)], axis=0)
                    else:
                        w = last.astype(BF)
                        part = jnp.sum(last, axis=0, keepdims=True)
                    t = mm(vt[:, kc * wide : kc * wide + wide], w)
                    lnum = t if lnum is None else lnum + t
                    lsum = part if lsum is None else lsum + part
                lnums.append(lnum)
                lsums.append(lsum)
        for r in range(rows // block):
            at = r * block
            mask = (band & ((key >= WINDOW) | present)) if r == 0 else band
            both = jnp.concatenate([q[at : at + block] for q in qs], axis=0)
            s = mm(kx[at : at + span], both, 1, 1)
            s = jnp.where(mask, s, -1e30)
            p = jnp.exp2((s - jnp.max(s, axis=0, keepdims=True)) * scale)
            wsum = jnp.sum(p, axis=0, keepdims=True)
            wnum = mm(vt[:, at : at + span], p.astype(BF))
            for k in range(2):
                mine = slice(k * block, (k + 1) * block)
                mixed = k * (rows // wide) + at // wide
                part = slice(at % wide, at % wide + block)
                num_ref[out + pair + k, :, at : at + block] = (
                    mixes[k] * wnum[:, mine] + rests[k] * lnums[mixed][:, part]
                )
                den_ref[out + pair + k, :, at : at + block] = (
                    mixes[k] * wsum[:, mine] + rests[k] * lsums[mixed][:, part]
                )


def finished(per_part, which, half, idx_ref, share_ref, held, pieces):
    at = pl.ds(pl.multiple_of(idx_ref[which] * half, 128), half)
    head = 0
    for num, den, qf in held:
        count, width, _ = num.shape
        for e in range(count):
            m = lax.bitwise_xor(idx_ref[0], head // per_part)
            state = pieces[0][head % per_part]
            for k in range(1, PART):
                state = jnp.where(m == k, pieces[k][head % per_part], state)
            rest = 1.0 - jax.nn.sigmoid(jnp.full((1, half), share_ref[head], F32))
            both = mm(state, qf[e, :, at])
            numer = num[e, :, at] + rest * both[:width]
            denom = den[e, :, at] + rest * (both[width : width + 1] + both[width + 1 : width + 2])
            yield head, (numer * (1.0 / denom)).astype(BF).T
            head += 1


def split_refs(refs):
    held = [refs[3 * k : 3 * k + 3] for k in range(3)]
    return held, refs[9 : 9 + PART]


def final_sent_kernel(per_part, half, idx_ref, share_ref, *refs):
    out_ref = refs[-1]
    for head, rows in finished(per_part, 3, half, idx_ref, share_ref, *split_refs(refs)):
        out_ref[head] = rows


def final_kept_kernel(per_part, half, idx_ref, share_ref, *refs):
    out_ref, kept, sems = refs[-3:]
    heads = kept.shape[0]
    copies = []
    for head, rows in finished(per_part, 2, half, idx_ref, share_ref, *split_refs(refs)):
        kept[head] = rows
        copies.append(pltpu.make_async_copy(kept.at[head], out_ref.at[heads * idx_ref[2] + head], sems.at[head]))
        copies[-1].start()
    for copy in copies:
        copy.wait()


def tails_kernel(k_ref, v_ref, out_ref, sems):
    rows = k_ref.shape[0]
    copies = [
        pltpu.make_async_copy(ref.at[pl.ds(rows - WINDOW, WINDOW)], out_ref.at[n], sems.at[n])
        for n, ref in enumerate((k_ref, v_ref))
    ]
    for copy in copies:
        copy.start()
    for copy in copies:
        copy.wait()


def place_kernel(idx_ref, got_ref, _, out_ref, sems):
    heads = got_ref.shape[0]
    copies = [
        pltpu.make_async_copy(got_ref.at[head], out_ref.at[heads * idx_ref[3] + head], sems.at[head])
        for head in range(heads)
    ]
    for copy in copies:
        copy.start()
    for copy in copies:
        copy.wait()


def per_device(queries, key_vectors, value_vectors, query_map, key_map, window_param):
    rows, heads, width = queries.shape
    groups = key_vectors.shape[1]
    group_size = heads // groups
    feat = query_map.shape[2]
    per_part = heads // PART
    tall = width + 8
    devices = lax.axis_size("seq")
    zs = devices // PART
    position = lax.axis_index("seq")
    core = lax.axis_index("head")
    me = position % PART
    idx = jnp.stack([me, position, core, 1 - core]).astype(jnp.int32)
    params = pltpu.CompilerParams(vmem_limit_bytes=LIMIT)
    smem = pl.BlockSpec(memory_space=pltpu.SMEM)
    anywhere = pl.BlockSpec(memory_space=pl.ANY)
    vmem = pl.BlockSpec(memory_space=pltpu.VMEM)
    query_map = query_map.transpose(0, 2, 1)
    key_map = key_map.transpose(0, 2, 1)

    def xor(x, m):
        return lax.ppermute(x, "seq", [(i, i ^ m) for i in range(devices)])

    def shift(x, by):
        return lax.ppermute(x, "seq", [(i, i + by) for i in range(devices - by)])

    tails = pl.pallas_call(
        tails_kernel,
        in_specs=[anywhere] * 2,
        out_specs=pl.BlockSpec(memory_space=pltpu.VMEM),
        out_shape=jax.ShapeDtypeStruct((2, WINDOW, groups, width), BF),
        scratch_shapes=[pltpu.SemaphoreType.DMA((2,))],
        compiler_params=params,
        name="tails",
    )(key_vectors, value_vectors)
    halo = shift(tails, 1)

    piece_shape = jax.ShapeDtypeStruct((per_part, tall, width), BF)
    grouped = jax.ShapeDtypeStruct((groups, rows, width), BF)
    own_feat, keys, values, *pieces = pl.pallas_call(
        functools.partial(state_kernel, per_part, group_size),
        in_specs=[smem] + [vmem] * 3,
        out_specs=[vmem] * (3 + PART),
        out_shape=[jax.ShapeDtypeStruct((heads, rows, width), BF), grouped, grouped] + [piece_shape] * PART,
        scratch_shapes=[pltpu.VMEM((groups, tall, rows), BF)],
        compiler_params=params,
        name="states",
    )(idx, key_vectors, value_vectors, key_map)
    q_wide, keys, values = pl.pallas_call(
        functools.partial(prepare_kernel, group_size),
        in_specs=[vmem] * 4,
        out_specs=[vmem] * 3,
        out_shape=[
            jax.ShapeDtypeStruct((groups, rows * group_size, width), F32),
            jax.ShapeDtypeStruct((groups, WINDOW + rows, width), BF),
            jax.ShapeDtypeStruct((groups, width, WINDOW + rows), BF),
        ],
        compiler_params=params,
        name="prepare",
    )(queries, keys, values, halo)

    def near(first, count, after):
        return pl.pallas_call(
            functools.partial(near_kernel, group_size, first, STEP),
            grid=(count // STEP,),
            in_specs=[smem, smem] + [vmem] * 6 + [anywhere] * len(after),
            out_specs=[vmem] * 3,
            scratch_shapes=[pltpu.VMEM((STEP, WINDOW + rows, 2 * feat), BF)],
            out_shape=[
                jax.ShapeDtypeStruct((count, width, rows), F32),
                jax.ShapeDtypeStruct((count, 1, rows), F32),
                jax.ShapeDtypeStruct((count, 2 * feat, rows), BF),
            ],
            compiler_params=params,
            cost_estimate=pl.CostEstimate(
                flops=count * 4 * 10**8, bytes_accessed=count * 10**6, transcendentals=count * 3 * 10**5
            ),
            name="near_%d" % first,
        )(idx, window_param, q_wide, keys, values, own_feat, query_map, key_map, *after)

    pieces = [pieces[0]] + [xor(pieces[m], m) for m in range(1, PART)]
    held = near(0, SPLIT[0], [])
    total = pl.pallas_call(
        total_kernel, in_specs=[vmem] * PART + [anywhere], out_specs=vmem, out_shape=piece_shape, compiler_params=params, name="totals"
    )(*pieces, held[1])
    held = list(held)
    if zs <= 4:
        earlier = [shift(total, PART * k) for k in range(1, zs)]
    else:
        columns = [[z * PART + k for z in range(zs)] for k in range(PART)]
        gathered = lax.all_gather(total, "seq", axis_index_groups=columns)
        below = jnp.arange(zs) < position // PART
        summed = jnp.sum(jnp.where(below[:, None, None, None], gathered.astype(F32), 0.0), axis=0)
        high = summed.astype(BF)
        earlier = [high, (summed - high.astype(F32)).astype(BF)]
    held += near(SPLIT[0], SPLIT[1] - SPLIT[0], [total])
    prefixes = pl.pallas_call(
        functools.partial(prefix_kernel, len(earlier)),
        in_specs=[smem] + [vmem] * (PART + len(earlier)) + [anywhere],
        out_specs=[vmem] * PART,
        out_shape=[piece_shape] * PART,
        compiler_params=params,
        name="prefixes",
    )(idx, *pieces, *earlier, held[4])
    prior = [prefixes[0]] + [xor(prefixes[m], m) for m in range(1, PART)]
    held += near(SPLIT[1], heads - SPLIT[1], [prefixes[0]])

    half = rows // 2
    theirs = pl.pallas_call(
        functools.partial(final_sent_kernel, per_part, half),
        in_specs=[smem, smem] + [vmem] * (9 + PART),
        out_specs=vmem,
        out_shape=jax.ShapeDtypeStruct((heads, half, width), BF),
        compiler_params=params,
        name="final_sent",
    )(idx, window_param, *held, *prior)
    got = lax.ppermute(theirs, "head", [(0, 1), (1, 0)])
    out = pl.pallas_call(
        functools.partial(final_kept_kernel, per_part, half),
        in_specs=[smem, smem] + [vmem] * (9 + PART) + [anywhere],
        out_specs=pl.BlockSpec(memory_space=pltpu.HBM),
        out_shape=jax.ShapeDtypeStruct((2 * heads, half, width), BF),
        scratch_shapes=[pltpu.VMEM((heads, half, width), BF), pltpu.SemaphoreType.DMA((heads,))],
        compiler_params=params,
        cost_estimate=pl.CostEstimate(flops=10**9, bytes_accessed=5 * 10**6, transcendentals=0),
        name="final_kept",
    )(idx, window_param, *held, *prior, theirs)
    return pl.pallas_call(
        place_kernel,
        in_specs=[smem, vmem, pl.BlockSpec(memory_space=pltpu.HBM)],
        out_specs=pl.BlockSpec(memory_space=pltpu.HBM),
        out_shape=jax.ShapeDtypeStruct(out.shape, BF),
        scratch_shapes=[pltpu.SemaphoreType.DMA((heads,))],
        input_output_aliases={2: 0},
        compiler_params=params,
        name="place",
    )(idx, got, out)


def solution(mesh):
    in_specs = (
        P("seq", "head", None),
        P("seq", "head", None),
        P("seq", "head", None),
        P("head", None, None),
        P("head", None, None),
        P("head"),
    )
    out_specs = P(None, ("seq", "head"), None)
    return jax.shard_map(
        per_device, mesh=mesh, in_specs=in_specs, out_specs=out_specs, check_vma=False
    )
```

```python
import functools

import jax
import jax.numpy as jnp
import numpy as np
from jax import lax
from jax.experimental import pallas as pl
from jax.experimental.pallas import tpu as pltpu
from jax.sharding import PartitionSpec as P

WINDOW = 64
PART = 4
BF = jnp.bfloat16
F32 = jnp.float32
LIMIT = 16 * 1024 * 1024
STEP = 2
SPLIT = 12


def mm(a, b, ca=1, cb=0):
    return lax.dot_general(a, b, (((ca,), (cb,)), ((), ())), preferred_element_type=F32)


def features_t(logits):
    top = jnp.max(logits, axis=0, keepdims=True)
    low = jnp.min(logits, axis=0, keepdims=True)
    up = jnp.exp(logits - top)
    down = jnp.exp(low - logits)
    up = up * (1.0 / jnp.sum(up, axis=0, keepdims=True))
    down = down * (1.0 / jnp.sum(down, axis=0, keepdims=True))
    return jnp.concatenate([up, down], axis=0).astype(BF)


def split_norm(state):
    width = state.shape[-1]
    norm = state[width : width + 1]
    high = norm.astype(BF).astype(F32)
    low = norm - high
    row = lax.broadcasted_iota(jnp.int32, (8, width), 0)
    tail = jnp.where(row == 0, high, jnp.where(row == 1, low, 0.0))
    return jnp.concatenate([state[:width], tail], axis=0).astype(BF)


def join_norm(piece):
    wide = piece.astype(F32)
    width = wide.shape[-1]
    norm = wide[width : width + 1] + wide[width + 1 : width + 2]
    row = lax.broadcasted_iota(jnp.int32, (8, width), 0)
    return jnp.concatenate([wide[:width], jnp.where(row == 0, norm, 0.0)], axis=0)


def values_with_one(values):
    row = lax.broadcasted_iota(jnp.int32, (8, values.shape[0]), 0)
    return jnp.concatenate([values.T, jnp.where(row == 0, 1.0, 0.0).astype(BF)], axis=0)


def quarter_states(m, per_part, group_size, idx_ref, k_ref, vt_ref, w_ref, feat_ref, out):
    head = lax.bitwise_xor(idx_ref[0], m) * per_part
    g = head // group_size
    logits = mm(w_ref[pl.ds(head, per_part)].reshape(-1, k_ref.shape[-1]), k_ref[g], 1, 1)
    f = w_ref.shape[1]
    for e in range(per_part):
        feat = features_t(logits[e * f : (e + 1) * f]).T
        feat_ref[head + e] = feat
        out[e] = split_norm(mm(vt_ref[g], feat))


def sent_states_kernel(
    per_part, group_size, idx_ref, k_hbm, v_hbm, w_hbm, feat_ref, kg_ref, vg_ref, vt_ref, p1, p2, p3,
    k_raw, v_raw, w_raw, sems,
):
    copies = [
        pltpu.make_async_copy(source, target, sems.at[n])
        for n, (source, target) in enumerate(((k_hbm, k_raw), (v_hbm, v_raw), (w_hbm, w_raw)))
    ]
    for copy in copies:
        copy.start()
    for copy in copies:
        copy.wait()
    rows, groups, _ = k_raw.shape
    wide_k = k_raw[...].astype(F32)
    wide_v = v_raw[...].astype(F32)
    for g in range(groups):
        kg_ref[g] = wide_k[:, g].astype(BF)
        values = wide_v[:, g].astype(BF)
        vg_ref[g] = values
        vt_ref[g] = values_with_one(values)
    for m, out in enumerate((p1, p2, p3), 1):
        quarter_states(m, per_part, group_size, idx_ref, kg_ref, vt_ref, w_raw, feat_ref, out)


def own_states_kernel(per_part, group_size, idx_ref, k_ref, v_ref, vt_ref, w_ref, _, feat_ref, out, tail_ref):
    rows = k_ref.shape[1]
    tail_ref[0] = k_ref[:, rows - WINDOW :]
    tail_ref[1] = v_ref[:, rows - WINDOW :]
    quarter_states(0, per_part, group_size, idx_ref, k_ref, vt_ref, w_ref, feat_ref, out)


def total_kernel(a, b, c, d, out):
    for e in range(out.shape[0]):
        out[e] = split_norm(join_norm(a[e]) + join_norm(b[e]) + join_norm(c[e]) + join_norm(d[e]))


def prefix_kernel(zs, idx_ref, *refs):
    own, outs = refs[:PART], refs[PART + zs + 1 :]
    me = idx_ref[0]
    for e in range(outs[0].shape[0]):
        base = jnp.zeros(own[0].shape[1:], F32)
        for k in range(zs):
            base = base + join_norm(refs[PART + k][e])
        terms = [join_norm(r[e]) for r in own]
        for m in range(PART):
            total = base
            for k in range(PART):
                earlier = lax.bitwise_xor(me, k) < lax.bitwise_xor(me, m)
                total = total + jnp.where(earlier, terms[k], 0.0)
            outs[m][e] = split_norm(total)


def prepare_kernel(group_size, q_ref, k_ref, v_ref, halo_ref, _, q_wide, kx, vt):
    rows, _, width = q_ref.shape
    for g in range(k_ref.shape[0]):
        q = q_ref[:, g * group_size : (g + 1) * group_size].astype(F32)
        q_wide[g] = q.reshape(rows * group_size, width)
        kx[g, :WINDOW] = halo_ref[0, g]
        kx[g, WINDOW:] = k_ref[g]
        vt[g] = jnp.concatenate([halo_ref[1, g], v_ref[g]], axis=0).T


def near_kernel(group_size, first, count, idx_ref, share_ref, q_wide, kx_ref, vt_ref, feat_ref, wq_ref, wk_ref, *refs):
    num_ref, den_ref, qf_ref, fx = refs[-4:]
    out = pl.program_id(0) * count
    head = first + out
    g = head // group_size
    rows, width = feat_ref.shape[1:]
    scale = np.float32(np.log2(np.e) / np.sqrt(width))
    kx, vt = kx_ref.at[g], vt_ref.at[g]
    present = idx_ref[1] > 0
    block = 128
    span = block + WINDOW
    key = lax.broadcasted_iota(jnp.int32, (span, 2 * block), 0)
    row = lax.broadcasted_iota(jnp.int32, (span, 2 * block), 1) % block
    band = (key > row) & (key <= row + WINDOW)
    wide = 2 * block
    causal = lax.broadcasted_iota(jnp.int32, (wide, wide), 0) <= lax.broadcasted_iota(jnp.int32, (wide, wide), 1)
    halo_logits = mm(wk_ref[pl.ds(head, count)].reshape(-1, width), kx[:128], 1, 1)
    feat = halo_logits.shape[0] // count
    for pair in range(0, count, 2):
        qs, mixes, rests, lnums, lsums = [], [], [], [], []
        for e in (pair, pair + 1):
            halo_feat = features_t(halo_logits[e * feat : (e + 1) * feat]).T[:WINDOW]
            fx[e, :WINDOW] = jnp.where(present, halo_feat.astype(F32), 0.0).astype(BF)
            fx[e, WINDOW:] = feat_ref[head + e]
            mixes.append(jax.nn.sigmoid(jnp.full((1, block), share_ref[head + e], F32)))
            rests.append(1.0 - mixes[-1])
            q = q_wide[g, pl.ds(head % group_size + e, rows, stride=group_size), :].astype(BF)
            qs.append(q)
            qf = features_t(mm(wq_ref[head + e], q, 1, 1))
            qf_ref[out + e] = qf
            for r in range(rows // wide):
                at = r * wide
                lnum = None
                lsum = None
                for kc in range(r + 1):
                    a = mm(fx[e, kc * wide : kc * wide + wide], qf[:, at : at + wide])
                    if kc == r:
                        last = jnp.where(causal, a, 0.0)
                    else:
                        last = a
                    if kc == 0:
                        halo = a[:WINDOW]
                        kept = halo.astype(BF).astype(F32)
                        body = last[WINDOW:]
                        part = jnp.sum(body, axis=0, keepdims=True)
                        if r == 0:
                            inside = causal[:WINDOW]
                            kept = jnp.where(inside, kept, 0.0)
                            part = part - jnp.sum(jnp.where(inside, 0.0, halo), axis=0, keepdims=True)
                        w = jnp.concatenate([(kept - halo).astype(BF), body.astype(BF)], axis=0)
                    else:
                        w = last.astype(BF)
                        part = jnp.sum(last, axis=0, keepdims=True)
                    t = mm(vt[:, kc * wide : kc * wide + wide], w)
                    lnum = t if lnum is None else lnum + t
                    lsum = part if lsum is None else lsum + part
                lnums.append(lnum)
                lsums.append(lsum)
        for r in range(rows // block):
            at = r * block
            mask = (band & ((key >= WINDOW) | present)) if r == 0 else band
            both = jnp.concatenate([q[at : at + block] for q in qs], axis=0)
            s = mm(kx[at : at + span], both, 1, 1)
            s = jnp.where(mask, s, -1e30)
            p = jnp.exp2((s - jnp.max(s, axis=0, keepdims=True)) * scale)
            wsum = jnp.sum(p, axis=0, keepdims=True)
            wnum = mm(vt[:, at : at + span], p.astype(BF))
            for k in range(2):
                mine = slice(k * block, (k + 1) * block)
                mixed = k * (rows // wide) + at // wide
                part = slice(at % wide, at % wide + block)
                num_ref[out + pair + k, :, at : at + block] = (
                    mixes[k] * wnum[:, mine] + rests[k] * lnums[mixed][:, part]
                )
                den_ref[out + pair + k, :, at : at + block] = (
                    mixes[k] * wsum[:, mine] + rests[k] * lsums[mixed][:, part]
                )


def finished(per_part, which, half, idx_ref, share_ref, held, pieces):
    at = pl.ds(pl.multiple_of(idx_ref[which] * half, 128), half)
    head = 0
    for num, den, qf in held:
        count, width, _ = num.shape
        for e in range(count):
            m = lax.bitwise_xor(idx_ref[0], head // per_part)
            state = pieces[0][head % per_part]
            for k in range(1, PART):
                state = jnp.where(m == k, pieces[k][head % per_part], state)
            rest = 1.0 - jax.nn.sigmoid(jnp.full((1, half), share_ref[head], F32))
            both = mm(state, qf[e, :, at])
            numer = num[e, :, at] + rest * both[:width]
            denom = den[e, :, at] + rest * (both[width : width + 1] + both[width + 1 : width + 2])
            yield head, (numer * (1.0 / denom)).astype(BF).T
            head += 1


def split_refs(refs):
    held = [refs[3 * k : 3 * k + 3] for k in range(2)]
    return held, refs[6 : 6 + PART]


def final_sent_kernel(per_part, half, idx_ref, share_ref, *refs):
    out_ref = refs[-1]
    for head, rows in finished(per_part, 3, half, idx_ref, share_ref, *split_refs(refs)):
        out_ref[head] = rows


def final_kept_kernel(per_part, half, idx_ref, share_ref, *refs):
    out_ref, kept, sems = refs[-3:]
    heads = kept.shape[0]
    copies = []
    for head, rows in finished(per_part, 2, half, idx_ref, share_ref, *split_refs(refs)):
        kept[head] = rows
        copies.append(pltpu.make_async_copy(kept.at[head], out_ref.at[heads * idx_ref[2] + head], sems.at[head]))
        copies[-1].start()
    for copy in copies:
        copy.wait()


def place_kernel(idx_ref, got_ref, _, out_ref, sems):
    heads = got_ref.shape[0]
    copies = [
        pltpu.make_async_copy(got_ref.at[head], out_ref.at[heads * idx_ref[3] + head], sems.at[head])
        for head in range(heads)
    ]
    for copy in copies:
        copy.start()
    for copy in copies:
        copy.wait()


def per_device(queries, key_vectors, value_vectors, query_map, key_map, window_param):
    rows, heads, width = queries.shape
    groups = key_vectors.shape[1]
    group_size = heads // groups
    feat = query_map.shape[2]
    per_part = heads // PART
    tall = width + 8
    devices = lax.axis_size("seq")
    zs = devices // PART
    position = lax.axis_index("seq")
    core = lax.axis_index("head")
    me = position % PART
    idx = jnp.stack([me, position, core, 1 - core]).astype(jnp.int32)
    params = pltpu.CompilerParams(vmem_limit_bytes=LIMIT)
    smem = pl.BlockSpec(memory_space=pltpu.SMEM)
    anywhere = pl.BlockSpec(memory_space=pl.ANY)
    vmem = pl.BlockSpec(memory_space=pltpu.VMEM)
    query_map = query_map.transpose(0, 2, 1)
    key_map = key_map.transpose(0, 2, 1)

    def xor(x, m):
        return lax.ppermute(x, "seq", [(i, i ^ m) for i in range(devices)])

    def shift(x, by):
        return lax.ppermute(x, "seq", [(i, i + by) for i in range(devices - by)])

    piece_shape = jax.ShapeDtypeStruct((per_part, tall, width), BF)
    grouped = jax.ShapeDtypeStruct((groups, rows, width), BF)
    feat_shape = jax.ShapeDtypeStruct((heads, rows, width), BF)
    hbm = pl.BlockSpec(memory_space=pltpu.HBM)
    own_feat, keys, values, values_t, *pieces = pl.pallas_call(
        functools.partial(sent_states_kernel, per_part, group_size),
        in_specs=[smem] + [hbm] * 3,
        out_specs=[vmem] * (4 + PART - 1),
        out_shape=[
            feat_shape,
            grouped,
            grouped,
            jax.ShapeDtypeStruct((groups, tall, rows), BF),
        ]
        + [piece_shape] * (PART - 1),
        scratch_shapes=[
            pltpu.VMEM((rows, groups, width), BF),
            pltpu.VMEM((rows, groups, width), BF),
            pltpu.VMEM(key_map.shape, BF),
            pltpu.SemaphoreType.DMA((3,)),
        ],
        compiler_params=params,
        name="sent_states",
    )(idx, *(pltpu.with_memory_space_constraint(x, pltpu.HBM) for x in (key_vectors, value_vectors, key_map)))
    pieces = [xor(pieces[m - 1], m) for m in range(1, PART)]
    own_feat, own_piece, tails = pl.pallas_call(
        functools.partial(own_states_kernel, per_part, group_size),
        in_specs=[smem] + [vmem] * 5,
        out_specs=[vmem] * 3,
        out_shape=[feat_shape, piece_shape, jax.ShapeDtypeStruct((2, groups, WINDOW, width), BF)],
        input_output_aliases={5: 0},
        compiler_params=params,
        cost_estimate=pl.CostEstimate(flops=10**9, bytes_accessed=2 * 10**6, transcendentals=10**6),
        name="own_states",
    )(idx, keys, values, values_t, key_map, own_feat)
    halo = shift(tails, 1)
    pieces = [own_piece] + pieces
    total = pl.pallas_call(
        total_kernel, in_specs=[vmem] * PART, out_specs=vmem, out_shape=piece_shape, compiler_params=params, name="totals"
    )(*pieces)
    if zs <= 4:
        earlier = [shift(total, PART * k) for k in range(1, zs)]
    else:
        columns = [[z * PART + k for z in range(zs)] for k in range(PART)]
        gathered = lax.all_gather(total, "seq", axis_index_groups=columns)
        below = jnp.arange(zs) < position // PART
        summed = jnp.sum(jnp.where(below[:, None, None, None], gathered.astype(F32), 0.0), axis=0)
        high = summed.astype(BF)
        earlier = [high, (summed - high.astype(F32)).astype(BF)]
    q_wide, keys, values = pl.pallas_call(
        functools.partial(prepare_kernel, group_size),
        in_specs=[vmem] * 4 + [anywhere],
        out_specs=[vmem] * 3,
        out_shape=[
            jax.ShapeDtypeStruct((groups, rows * group_size, width), F32),
            jax.ShapeDtypeStruct((groups, WINDOW + rows, width), BF),
            jax.ShapeDtypeStruct((groups, width, WINDOW + rows), BF),
        ],
        compiler_params=params,
        name="prepare",
    )(queries, keys, values, halo, total)

    def near(first, count, after):
        return pl.pallas_call(
            functools.partial(near_kernel, group_size, first, STEP),
            grid=(count // STEP,),
            in_specs=[smem, smem] + [vmem] * 6 + [anywhere] * len(after),
            out_specs=[vmem] * 3,
            scratch_shapes=[pltpu.VMEM((STEP, WINDOW + rows, 2 * feat), BF)],
            out_shape=[
                jax.ShapeDtypeStruct((count, width, rows), F32),
                jax.ShapeDtypeStruct((count, 1, rows), F32),
                jax.ShapeDtypeStruct((count, 2 * feat, rows), BF),
            ],
            compiler_params=params,
            cost_estimate=pl.CostEstimate(
                flops=count * 4 * 10**8, bytes_accessed=count * 10**6, transcendentals=count * 3 * 10**5
            ),
            name="near_%d" % first,
        )(idx, window_param, q_wide, keys, values, own_feat, query_map, key_map, *after)

    held = list(near(0, SPLIT, []))
    prefixes = pl.pallas_call(
        functools.partial(prefix_kernel, len(earlier)),
        in_specs=[smem] + [vmem] * (PART + len(earlier)) + [anywhere],
        out_specs=[vmem] * PART,
        out_shape=[piece_shape] * PART,
        compiler_params=params,
        name="prefixes",
    )(idx, *pieces, *earlier, held[1])
    prior = [prefixes[0]] + [xor(prefixes[m], m) for m in range(1, PART)]
    held += near(SPLIT, heads - SPLIT, [prefixes[0]])

    half = rows // 2
    theirs = pl.pallas_call(
        functools.partial(final_sent_kernel, per_part, half),
        in_specs=[smem, smem] + [vmem] * (6 + PART),
        out_specs=vmem,
        out_shape=jax.ShapeDtypeStruct((heads, half, width), BF),
        compiler_params=params,
        name="final_sent",
    )(idx, window_param, *held, *prior)
    got = lax.ppermute(theirs, "head", [(0, 1), (1, 0)])
    out = pl.pallas_call(
        functools.partial(final_kept_kernel, per_part, half),
        in_specs=[smem, smem] + [vmem] * (6 + PART) + [anywhere],
        out_specs=pl.BlockSpec(memory_space=pltpu.HBM),
        out_shape=jax.ShapeDtypeStruct((2 * heads, half, width), BF),
        scratch_shapes=[pltpu.VMEM((heads, half, width), BF), pltpu.SemaphoreType.DMA((heads,))],
        compiler_params=params,
        cost_estimate=pl.CostEstimate(flops=10**9, bytes_accessed=5 * 10**6, transcendentals=0),
        name="final_kept",
    )(idx, window_param, *held, *prior, theirs)
    return pl.pallas_call(
        place_kernel,
        in_specs=[smem, vmem, pl.BlockSpec(memory_space=pltpu.HBM)],
        out_specs=pl.BlockSpec(memory_space=pltpu.HBM),
        out_shape=jax.ShapeDtypeStruct(out.shape, BF),
        scratch_shapes=[pltpu.SemaphoreType.DMA((heads,))],
        input_output_aliases={2: 0},
        compiler_params=params,
        name="place",
    )(idx, got, out)


def solution(mesh):
    in_specs = (
        P("seq", "head", None),
        P("seq", "head", None),
        P("seq", "head", None),
        P("head", None, None),
        P("head", None, None),
        P("head"),
    )
    out_specs = P(None, ("seq", "head"), None)
    return jax.shard_map(
        per_device, mesh=mesh, in_specs=in_specs, out_specs=out_specs, check_vma=False
    )
```

```python
import functools

import jax
import jax.numpy as jnp
import numpy as np
from jax import lax
from jax.experimental import pallas as pl
from jax.experimental.pallas import tpu as pltpu
from jax.sharding import PartitionSpec as P

WINDOW = 64
PART = 4
BF = jnp.bfloat16
F32 = jnp.float32
LIMIT = 16 * 1024 * 1024
STEP = 4
SPLIT = 12


def mm(a, b, ca=1, cb=0):
    return lax.dot_general(a, b, (((ca,), (cb,)), ((), ())), preferred_element_type=F32)


def features_t(logits):
    top = jnp.max(logits, axis=0, keepdims=True)
    low = jnp.min(logits, axis=0, keepdims=True)
    up = jnp.exp(logits - top)
    down = jnp.exp(low - logits)
    up = up * (1.0 / jnp.sum(up, axis=0, keepdims=True))
    down = down * (1.0 / jnp.sum(down, axis=0, keepdims=True))
    return jnp.concatenate([up, down], axis=0).astype(BF)


def split_norm(state):
    width = state.shape[-1]
    norm = state[width : width + 1]
    high = norm.astype(BF).astype(F32)
    low = norm - high
    row = lax.broadcasted_iota(jnp.int32, (8, width), 0)
    tail = jnp.where(row == 0, high, jnp.where(row == 1, low, 0.0))
    return jnp.concatenate([state[:width], tail], axis=0).astype(BF)


def join_norm(piece):
    wide = piece.astype(F32)
    width = wide.shape[-1]
    norm = wide[width : width + 1] + wide[width + 1 : width + 2]
    row = lax.broadcasted_iota(jnp.int32, (8, width), 0)
    return jnp.concatenate([wide[:width], jnp.where(row == 0, norm, 0.0)], axis=0)


def values_with_one(values):
    row = lax.broadcasted_iota(jnp.int32, (8, values.shape[0]), 0)
    return jnp.concatenate([values.T, jnp.where(row == 0, 1.0, 0.0).astype(BF)], axis=0)


def quarter_states(m, per_part, group_size, idx_ref, k_ref, vt_ref, w_ref, feat_ref, out):
    head = lax.bitwise_xor(idx_ref[0], m) * per_part
    g = head // group_size
    logits = mm(w_ref[pl.ds(head, per_part)].reshape(-1, k_ref.shape[-1]), k_ref[g], 1, 1)
    f = w_ref.shape[1]
    for e in range(per_part):
        feat = features_t(logits[e * f : (e + 1) * f]).T
        feat_ref[head + e] = feat
        out[e] = split_norm(mm(vt_ref[g], feat))


def sent_states_kernel(
    per_part, group_size, idx_ref, k_hbm, v_hbm, w_hbm, feat_ref, kg_ref, vg_ref, vt_ref, p1, p2, p3,
    k_raw, v_raw, w_raw, sems,
):
    copies = [
        pltpu.make_async_copy(source, target, sems.at[n])
        for n, (source, target) in enumerate(((k_hbm, k_raw), (v_hbm, v_raw), (w_hbm, w_raw)))
    ]
    for copy in copies:
        copy.start()
    for copy in copies:
        copy.wait()
    rows, groups, _ = k_raw.shape
    wide_k = k_raw[...].astype(F32)
    wide_v = v_raw[...].astype(F32)
    for g in range(groups):
        kg_ref[g] = wide_k[:, g].astype(BF)
        values = wide_v[:, g].astype(BF)
        vg_ref[g] = values
        vt_ref[g] = values_with_one(values)
    for m, out in enumerate((p1, p2, p3), 1):
        quarter_states(m, per_part, group_size, idx_ref, kg_ref, vt_ref, w_raw, feat_ref, out)


def own_states_kernel(per_part, group_size, idx_ref, k_ref, v_ref, vt_ref, w_ref, _, feat_ref, out, tail_ref):
    rows = k_ref.shape[1]
    tail_ref[0] = k_ref[:, rows - WINDOW :]
    tail_ref[1] = v_ref[:, rows - WINDOW :]
    quarter_states(0, per_part, group_size, idx_ref, k_ref, vt_ref, w_ref, feat_ref, out)


def total_kernel(a, b, c, d, out):
    for e in range(out.shape[0]):
        out[e] = split_norm(join_norm(a[e]) + join_norm(b[e]) + join_norm(c[e]) + join_norm(d[e]))


def prefix_kernel(zs, idx_ref, *refs):
    own, outs = refs[:PART], refs[PART + zs + 1 :]
    me = idx_ref[0]
    for e in range(outs[0].shape[0]):
        base = jnp.zeros(own[0].shape[1:], F32)
        for k in range(zs):
            base = base + join_norm(refs[PART + k][e])
        terms = [join_norm(r[e]) for r in own]
        for m in range(PART):
            total = base
            for k in range(PART):
                earlier = lax.bitwise_xor(me, k) < lax.bitwise_xor(me, m)
                total = total + jnp.where(earlier, terms[k], 0.0)
            outs[m][e] = split_norm(total)


def prepare_kernel(group_size, q_ref, k_ref, v_ref, halo_ref, _, q_wide, kx, vt):
    rows, _, width = q_ref.shape
    for g in range(k_ref.shape[0]):
        q = q_ref[:, g * group_size : (g + 1) * group_size].astype(F32)
        q_wide[g] = q.reshape(rows * group_size, width)
        kx[g, :WINDOW] = halo_ref[0, g]
        kx[g, WINDOW:] = k_ref[g]
        vt[g] = jnp.concatenate([halo_ref[1, g], v_ref[g]], axis=0).T


def near_kernel(group_size, first, count, idx_ref, share_ref, q_wide, kx_ref, vt_ref, feat_ref, wq_ref, wk_ref, *refs):
    num_ref, den_ref, qf_ref, fx = refs[-4:]
    out = pl.program_id(0) * count
    head = first + out
    g = head // group_size
    rows, width = feat_ref.shape[1:]
    scale = np.float32(np.log2(np.e) / np.sqrt(width))
    kx, vt = kx_ref.at[g], vt_ref.at[g]
    present = idx_ref[1] > 0
    block = 128
    span = block + WINDOW
    key = lax.broadcasted_iota(jnp.int32, (span, 2 * block), 0)
    row = lax.broadcasted_iota(jnp.int32, (span, 2 * block), 1) % block
    band = (key > row) & (key <= row + WINDOW)
    wide = 2 * block
    causal = lax.broadcasted_iota(jnp.int32, (wide, wide), 0) <= lax.broadcasted_iota(jnp.int32, (wide, wide), 1)
    halo_logits = mm(wk_ref[pl.ds(head, count)].reshape(-1, width), kx[:128], 1, 1)
    feat = halo_logits.shape[0] // count
    for pair in range(0, count, 2):
        qs, mixes, rests, lnums, lsums = [], [], [], [], []
        products, logits = [], [[], []]
        for r in range(rows // block):
            at = r * block
            both = jnp.concatenate(
                [
                    q_wide[g, pl.ds(at * group_size + head % group_size + e, block, stride=group_size), :].astype(BF)
                    for e in (pair, pair + 1)
                ],
                axis=0,
            )
            maps = [wq_ref[head + pair], wq_ref[head + pair + 1], kx[at : at + span]]
            x = mm(jnp.concatenate(maps, axis=0), both, 1, 1)
            logits[0].append(x[:feat, :block])
            logits[1].append(x[feat : 2 * feat, block:])
            products.append(x[2 * feat :])
        for e in (pair, pair + 1):
            halo_feat = features_t(halo_logits[e * feat : (e + 1) * feat]).T[:WINDOW]
            fx[e, :WINDOW] = jnp.where(present, halo_feat.astype(F32), 0.0).astype(BF)
            fx[e, WINDOW:] = feat_ref[head + e]
            mixes.append(jax.nn.sigmoid(jnp.full((1, block), share_ref[head + e], F32)))
            rests.append(1.0 - mixes[-1])
            qf = features_t(jnp.concatenate(logits[e - pair], axis=1))
            qf_ref[out + e] = qf
            for r in range(rows // wide):
                at = r * wide
                lnum = None
                lsum = None
                for kc in range(r + 1):
                    a = mm(fx[e, kc * wide : kc * wide + wide], qf[:, at : at + wide])
                    if kc == r:
                        last = jnp.where(causal, a, 0.0)
                    else:
                        last = a
                    if kc == 0:
                        halo = a[:WINDOW]
                        kept = halo.astype(BF).astype(F32)
                        body = last[WINDOW:]
                        part = jnp.sum(body, axis=0, keepdims=True)
                        if r == 0:
                            inside = causal[:WINDOW]
                            kept = jnp.where(inside, kept, 0.0)
                            part = part - jnp.sum(jnp.where(inside, 0.0, halo), axis=0, keepdims=True)
                        w = jnp.concatenate([(kept - halo).astype(BF), body.astype(BF)], axis=0)
                    else:
                        w = last.astype(BF)
                        part = jnp.sum(last, axis=0, keepdims=True)
                    t = mm(vt[:, kc * wide : kc * wide + wide], w)
                    lnum = t if lnum is None else lnum + t
                    lsum = part if lsum is None else lsum + part
                lnums.append(lnum)
                lsums.append(lsum)
        for r in range(rows // block):
            at = r * block
            mask = (band & ((key >= WINDOW) | present)) if r == 0 else band
            s = jnp.where(mask, products[r], -1e30)
            p = jnp.exp2((s - jnp.max(s, axis=0, keepdims=True)) * scale)
            wsum = jnp.sum(p, axis=0, keepdims=True)
            wnum = mm(vt[:, at : at + span], p.astype(BF))
            for k in range(2):
                mine = slice(k * block, (k + 1) * block)
                mixed = k * (rows // wide) + at // wide
                part = slice(at % wide, at % wide + block)
                num_ref[out + pair + k, :, at : at + block] = (
                    mixes[k] * wnum[:, mine] + rests[k] * lnums[mixed][:, part]
                )
                den_ref[out + pair + k, :, at : at + block] = (
                    mixes[k] * wsum[:, mine] + rests[k] * lsums[mixed][:, part]
                )


def finished(per_part, which, half, idx_ref, share_ref, held, pieces):
    at = pl.ds(pl.multiple_of(idx_ref[which] * half, 128), half)
    head = 0
    for num, den, qf in held:
        count, width, _ = num.shape
        for e in range(count):
            m = lax.bitwise_xor(idx_ref[0], head // per_part)
            state = pieces[0][head % per_part]
            for k in range(1, PART):
                state = jnp.where(m == k, pieces[k][head % per_part], state)
            rest = 1.0 - jax.nn.sigmoid(jnp.full((1, half), share_ref[head], F32))
            both = mm(state, qf[e, :, at])
            numer = num[e, :, at] + rest * both[:width]
            denom = den[e, :, at] + rest * (both[width : width + 1] + both[width + 1 : width + 2])
            yield head, (numer * (1.0 / denom)).astype(BF).T
            head += 1


def split_refs(refs):
    held = [refs[3 * k : 3 * k + 3] for k in range(2)]
    return held, refs[6 : 6 + PART]


def final_sent_kernel(per_part, half, idx_ref, share_ref, *refs):
    out_ref = refs[-1]
    for head, rows in finished(per_part, 3, half, idx_ref, share_ref, *split_refs(refs)):
        out_ref[head] = rows


def final_kept_kernel(per_part, half, idx_ref, share_ref, *refs):
    out_ref, kept, sems = refs[-3:]
    heads = kept.shape[0]
    copies = []
    for head, rows in finished(per_part, 2, half, idx_ref, share_ref, *split_refs(refs)):
        kept[head] = rows
        copies.append(pltpu.make_async_copy(kept.at[head], out_ref.at[heads * idx_ref[2] + head], sems.at[head]))
        copies[-1].start()
    for copy in copies:
        copy.wait()


def place_kernel(idx_ref, got_ref, _, out_ref, sems):
    heads = got_ref.shape[0]
    copies = [
        pltpu.make_async_copy(got_ref.at[head], out_ref.at[heads * idx_ref[3] + head], sems.at[head])
        for head in range(heads)
    ]
    for copy in copies:
        copy.start()
    for copy in copies:
        copy.wait()


def per_device(queries, key_vectors, value_vectors, query_map, key_map, window_param):
    rows, heads, width = queries.shape
    groups = key_vectors.shape[1]
    group_size = heads // groups
    feat = query_map.shape[2]
    per_part = heads // PART
    tall = width + 8
    devices = lax.axis_size("seq")
    zs = devices // PART
    position = lax.axis_index("seq")
    core = lax.axis_index("head")
    me = position % PART
    idx = jnp.stack([me, position, core, 1 - core]).astype(jnp.int32)
    params = pltpu.CompilerParams(vmem_limit_bytes=LIMIT)
    smem = pl.BlockSpec(memory_space=pltpu.SMEM)
    anywhere = pl.BlockSpec(memory_space=pl.ANY)
    vmem = pl.BlockSpec(memory_space=pltpu.VMEM)
    query_map = query_map.transpose(0, 2, 1)
    key_map = key_map.transpose(0, 2, 1)

    def xor(x, m):
        return lax.ppermute(x, "seq", [(i, i ^ m) for i in range(devices)])

    def shift(x, by):
        return lax.ppermute(x, "seq", [(i, i + by) for i in range(devices - by)])

    piece_shape = jax.ShapeDtypeStruct((per_part, tall, width), BF)
    grouped = jax.ShapeDtypeStruct((groups, rows, width), BF)
    feat_shape = jax.ShapeDtypeStruct((heads, rows, width), BF)
    hbm = pl.BlockSpec(memory_space=pltpu.HBM)
    own_feat, keys, values, values_t, *pieces = pl.pallas_call(
        functools.partial(sent_states_kernel, per_part, group_size),
        in_specs=[smem] + [hbm] * 3,
        out_specs=[vmem] * (4 + PART - 1),
        out_shape=[
            feat_shape,
            grouped,
            grouped,
            jax.ShapeDtypeStruct((groups, tall, rows), BF),
        ]
        + [piece_shape] * (PART - 1),
        scratch_shapes=[
            pltpu.VMEM((rows, groups, width), BF),
            pltpu.VMEM((rows, groups, width), BF),
            pltpu.VMEM(key_map.shape, BF),
            pltpu.SemaphoreType.DMA((3,)),
        ],
        compiler_params=params,
        name="sent_states",
    )(idx, *(pltpu.with_memory_space_constraint(x, pltpu.HBM) for x in (key_vectors, value_vectors, key_map)))
    pieces = [xor(pieces[m - 1], m) for m in range(1, PART)]
    own_feat, own_piece, tails = pl.pallas_call(
        functools.partial(own_states_kernel, per_part, group_size),
        in_specs=[smem] + [vmem] * 5,
        out_specs=[vmem] * 3,
        out_shape=[feat_shape, piece_shape, jax.ShapeDtypeStruct((2, groups, WINDOW, width), BF)],
        input_output_aliases={5: 0},
        compiler_params=params,
        cost_estimate=pl.CostEstimate(flops=10**9, bytes_accessed=2 * 10**6, transcendentals=10**6),
        name="own_states",
    )(idx, keys, values, values_t, key_map, own_feat)
    halo = shift(tails, 1)
    pieces = [own_piece] + pieces
    total = pl.pallas_call(
        total_kernel, in_specs=[vmem] * PART, out_specs=vmem, out_shape=piece_shape, compiler_params=params, name="totals"
    )(*pieces)
    if zs <= 4:
        earlier = [shift(total, PART * k) for k in range(1, zs)]
    else:
        columns = [[z * PART + k for z in range(zs)] for k in range(PART)]
        gathered = lax.all_gather(total, "seq", axis_index_groups=columns)
        below = jnp.arange(zs) < position // PART
        summed = jnp.sum(jnp.where(below[:, None, None, None], gathered.astype(F32), 0.0), axis=0)
        high = summed.astype(BF)
        earlier = [high, (summed - high.astype(F32)).astype(BF)]
    q_wide, keys, values = pl.pallas_call(
        functools.partial(prepare_kernel, group_size),
        in_specs=[vmem] * 4 + [anywhere],
        out_specs=[vmem] * 3,
        out_shape=[
            jax.ShapeDtypeStruct((groups, rows * group_size, width), F32),
            jax.ShapeDtypeStruct((groups, WINDOW + rows, width), BF),
            jax.ShapeDtypeStruct((groups, width, WINDOW + rows), BF),
        ],
        compiler_params=params,
        name="prepare",
    )(queries, keys, values, halo, total)

    def near(first, count, after):
        return pl.pallas_call(
            functools.partial(near_kernel, group_size, first, STEP),
            grid=(count // STEP,),
            in_specs=[smem, smem] + [vmem] * 6 + [anywhere] * len(after),
            out_specs=[vmem] * 3,
            scratch_shapes=[pltpu.VMEM((STEP, WINDOW + rows, 2 * feat), BF)],
            out_shape=[
                jax.ShapeDtypeStruct((count, width, rows), F32),
                jax.ShapeDtypeStruct((count, 1, rows), F32),
                jax.ShapeDtypeStruct((count, 2 * feat, rows), BF),
            ],
            compiler_params=params,
            cost_estimate=pl.CostEstimate(
                flops=count * 4 * 10**8, bytes_accessed=count * 10**6, transcendentals=count * 3 * 10**5
            ),
            name="near_%d" % first,
        )(idx, window_param, q_wide, keys, values, own_feat, query_map, key_map, *after)

    held = list(near(0, SPLIT, []))
    prefixes = pl.pallas_call(
        functools.partial(prefix_kernel, len(earlier)),
        in_specs=[smem] + [vmem] * (PART + len(earlier)) + [anywhere],
        out_specs=[vmem] * PART,
        out_shape=[piece_shape] * PART,
        compiler_params=params,
        name="prefixes",
    )(idx, *pieces, *earlier, held[1])
    prior = [prefixes[0]] + [xor(prefixes[m], m) for m in range(1, PART)]
    held += near(SPLIT, heads - SPLIT, [prefixes[0]])

    half = rows // 2
    theirs = pl.pallas_call(
        functools.partial(final_sent_kernel, per_part, half),
        in_specs=[smem, smem] + [vmem] * (6 + PART),
        out_specs=vmem,
        out_shape=jax.ShapeDtypeStruct((heads, half, width), BF),
        compiler_params=params,
        name="final_sent",
    )(idx, window_param, *held, *prior)
    got = lax.ppermute(theirs, "head", [(0, 1), (1, 0)])
    out = pl.pallas_call(
        functools.partial(final_kept_kernel, per_part, half),
        in_specs=[smem, smem] + [vmem] * (6 + PART) + [anywhere],
        out_specs=pl.BlockSpec(memory_space=pltpu.HBM),
        out_shape=jax.ShapeDtypeStruct((2 * heads, half, width), BF),
        scratch_shapes=[pltpu.VMEM((heads, half, width), BF), pltpu.SemaphoreType.DMA((heads,))],
        compiler_params=params,
        cost_estimate=pl.CostEstimate(flops=10**9, bytes_accessed=5 * 10**6, transcendentals=0),
        name="final_kept",
    )(idx, window_param, *held, *prior, theirs)
    return pl.pallas_call(
        place_kernel,
        in_specs=[smem, vmem, pl.BlockSpec(memory_space=pltpu.HBM)],
        out_specs=pl.BlockSpec(memory_space=pltpu.HBM),
        out_shape=jax.ShapeDtypeStruct(out.shape, BF),
        scratch_shapes=[pltpu.SemaphoreType.DMA((heads,))],
        input_output_aliases={2: 0},
        compiler_params=params,
        name="place",
    )(idx, got, out)


def solution(mesh):
    in_specs = (
        P("seq", "head", None),
        P("seq", "head", None),
        P("seq", "head", None),
        P("head", None, None),
        P("head", None, None),
        P("head"),
    )
    out_specs = P(None, ("seq", "head"), None)
    return jax.shard_map(
        per_device, mesh=mesh, in_specs=in_specs, out_specs=out_specs, check_vma=False
    )
```

```python
import functools

import jax
import jax.numpy as jnp
import numpy as np
from jax import lax
from jax.experimental import pallas as pl
from jax.experimental.pallas import tpu as pltpu
from jax.sharding import PartitionSpec as P

WINDOW = 64
PART = 4
BF = jnp.bfloat16
F32 = jnp.float32
LIMIT = 16 * 1024 * 1024
STEP = 4
SPLIT = 12


def mm(a, b, ca=1, cb=0):
    return lax.dot_general(a, b, (((ca,), (cb,)), ((), ())), preferred_element_type=F32)


def features_t(logits):
    top = jnp.max(logits, axis=0, keepdims=True)
    low = jnp.min(logits, axis=0, keepdims=True)
    up = jnp.exp(logits - top)
    down = jnp.exp(low - logits)
    up = up * (1.0 / jnp.sum(up, axis=0, keepdims=True))
    down = down * (1.0 / jnp.sum(down, axis=0, keepdims=True))
    return jnp.concatenate([up, down], axis=0).astype(BF)


def put_state(ref, e, state, norm):
    width = state.shape[-1]
    high = norm.astype(BF).astype(F32)
    row = lax.broadcasted_iota(jnp.int32, (8, width), 0)
    ref[e, :width] = state.astype(BF)
    ref[e, width:] = jnp.where(row == 0, high, jnp.where(row == 1, norm - high, 0.0)).astype(BF)


def get_state(ref, e):
    width = ref.shape[-1]
    last = ref[e, width:].astype(F32)
    return ref[e, :width].astype(F32), last[0:1] + last[1:2]


def values_with_one(values):
    row = lax.broadcasted_iota(jnp.int32, (8, values.shape[0]), 0)
    return jnp.concatenate([values.T, jnp.where(row == 0, 1.0, 0.0).astype(BF)], axis=0)


def quarter_states(m, per_part, group_size, idx_ref, k_ref, vt_ref, w_ref, feat_ref, out):
    head = lax.bitwise_xor(idx_ref[0], m) * per_part
    g = head // group_size
    logits = mm(w_ref[pl.ds(head, per_part)].reshape(-1, k_ref.shape[-1]), k_ref[g], 1, 1)
    f = w_ref.shape[1]
    for e in range(per_part):
        feat = features_t(logits[e * f : (e + 1) * f]).T
        feat_ref[head + e] = feat
        state = mm(vt_ref[g], feat)
        width = state.shape[-1]
        put_state(out, e, state[:width], state[width : width + 1])


def sent_states_kernel(
    per_part, group_size, idx_ref, k_hbm, v_hbm, w_hbm, feat_ref, kg_ref, vg_ref, vt_ref, p1, p2, p3,
    k_raw, v_raw, w_raw, sems,
):
    copies = [
        pltpu.make_async_copy(source, target, sems.at[n])
        for n, (source, target) in enumerate(((k_hbm, k_raw), (v_hbm, v_raw), (w_hbm, w_raw)))
    ]
    for copy in copies:
        copy.start()
    for copy in copies:
        copy.wait()
    rows, groups, _ = k_raw.shape
    wide_k = k_raw[...].astype(F32)
    wide_v = v_raw[...].astype(F32)
    for g in range(groups):
        kg_ref[g] = wide_k[:, g].astype(BF)
        values = wide_v[:, g].astype(BF)
        vg_ref[g] = values
        vt_ref[g] = values_with_one(values)
    for m, out in enumerate((p1, p2, p3), 1):
        quarter_states(m, per_part, group_size, idx_ref, kg_ref, vt_ref, w_raw, feat_ref, out)


def own_states_kernel(per_part, group_size, idx_ref, k_ref, v_ref, vt_ref, w_ref, _, feat_ref, out, tail_ref):
    rows = k_ref.shape[1]
    tail_ref[0] = k_ref[:, rows - WINDOW :]
    tail_ref[1] = v_ref[:, rows - WINDOW :]
    quarter_states(0, per_part, group_size, idx_ref, k_ref, vt_ref, w_ref, feat_ref, out)


def total_kernel(a, b, c, d, out):
    for e in range(out.shape[0]):
        states, norms = zip(*(get_state(ref, e) for ref in (a, b, c, d)))
        put_state(out, e, sum(states[1:], states[0]), sum(norms[1:], norms[0]))


def prefix_kernel(zs, exchanged, idx_ref, *refs):
    layer = idx_ref[1] // PART
    own, later, outs = refs[:PART], refs[PART : PART + zs], refs[PART + zs + 1 :]
    me = idx_ref[0]
    for e in range(outs[0].shape[0]):
        base = None
        for k, ref in enumerate(later, 1):
            term = get_state(ref, e)
            if exchanged:
                term = tuple(jnp.where(lax.bitwise_xor(layer, k) < layer, x, 0.0) for x in term)
            base = term if base is None else (base[0] + term[0], base[1] + term[1])
        terms = [get_state(ref, e) for ref in own]
        for m in range(PART):
            total = base
            for k in range(PART):
                if k != m:
                    earlier = lax.bitwise_xor(me, k) < lax.bitwise_xor(me, m)
                    total = tuple(t + jnp.where(earlier, x, 0.0) for t, x in zip(total, terms[k]))
            put_state(outs[m], e, *total)


def prepare_kernel(group_size, q_ref, k_ref, v_ref, halo_ref, _, q_wide, kx, vt):
    rows, _, width = q_ref.shape
    for g in range(k_ref.shape[0]):
        q = q_ref[:, g * group_size : (g + 1) * group_size].astype(F32)
        q_wide[g] = q.reshape(rows * group_size, width)
        kx[g, :WINDOW] = halo_ref[0, g]
        kx[g, WINDOW:] = k_ref[g]
        vt[g] = jnp.concatenate([halo_ref[1, g], v_ref[g]], axis=0).T


def near_kernel(group_size, per_part, first, count, idx_ref, share_ref, q_wide, kx_ref, vt_ref, feat_ref, wq_ref, wk_ref, *refs):
    num_ref, den_ref, qf_ref, fx = refs[-4:]
    out = pl.program_id(0) * count
    slot = first + out
    head = lax.bitwise_xor(idx_ref[0], slot // per_part) * per_part + slot % per_part
    g = head // group_size
    rows, width = feat_ref.shape[1:]
    scale = np.float32(np.log2(np.e) / np.sqrt(width))
    kx, vt = kx_ref.at[g], vt_ref.at[g]
    present = idx_ref[1] > 0
    block = 128
    span = block + WINDOW
    key = lax.broadcasted_iota(jnp.int32, (span, 2 * block), 0)
    row = lax.broadcasted_iota(jnp.int32, (span, 2 * block), 1) % block
    band = (key > row) & (key <= row + WINDOW)
    wide = 2 * block
    causal = lax.broadcasted_iota(jnp.int32, (wide, wide), 0) <= lax.broadcasted_iota(jnp.int32, (wide, wide), 1)
    halo_logits = mm(wk_ref[pl.ds(head, count)].reshape(-1, width), kx[:128], 1, 1)
    feat = halo_logits.shape[0] // count
    for pair in range(0, count, 2):
        qs, mixes, rests, lnums, lsums = [], [], [], [], []
        products, logits = [], [[], []]
        for r in range(rows // block):
            at = r * block
            both = jnp.concatenate(
                [
                    q_wide[g, pl.ds(at * group_size + head % group_size + e, block, stride=group_size), :].astype(BF)
                    for e in (pair, pair + 1)
                ],
                axis=0,
            )
            maps = [wq_ref[head + pair], wq_ref[head + pair + 1], kx[at : at + span]]
            x = mm(jnp.concatenate(maps, axis=0), both, 1, 1)
            logits[0].append(x[:feat, :block])
            logits[1].append(x[feat : 2 * feat, block:])
            products.append(x[2 * feat :])
        for e in (pair, pair + 1):
            halo_feat = features_t(halo_logits[e * feat : (e + 1) * feat]).T[:WINDOW]
            fx[e, :WINDOW] = jnp.where(present, halo_feat.astype(F32), 0.0).astype(BF)
            fx[e, WINDOW:] = feat_ref[head + e]
            mixes.append(jax.nn.sigmoid(jnp.full((1, block), share_ref[head + e], F32)))
            rests.append(1.0 - mixes[-1])
            qf = features_t(jnp.concatenate(logits[e - pair], axis=1))
            qf_ref[out + e] = qf
            for r in range(rows // wide):
                at = r * wide
                lnum = None
                lsum = None
                for kc in range(r + 1):
                    a = mm(fx[e, kc * wide : kc * wide + wide], qf[:, at : at + wide])
                    if kc == r:
                        last = jnp.where(causal, a, 0.0)
                    else:
                        last = a
                    if kc == 0:
                        halo = a[:WINDOW]
                        kept = halo.astype(BF).astype(F32)
                        body = last[WINDOW:]
                        part = jnp.sum(body, axis=0, keepdims=True)
                        if r == 0:
                            inside = causal[:WINDOW]
                            kept = jnp.where(inside, kept, 0.0)
                            part = part - jnp.sum(jnp.where(inside, 0.0, halo), axis=0, keepdims=True)
                        w = jnp.concatenate([(kept - halo).astype(BF), body.astype(BF)], axis=0)
                    else:
                        w = last.astype(BF)
                        part = jnp.sum(last, axis=0, keepdims=True)
                    t = mm(vt[:, kc * wide : kc * wide + wide], w)
                    lnum = t if lnum is None else lnum + t
                    lsum = part if lsum is None else lsum + part
                lnums.append(lnum)
                lsums.append(lsum)
        for r in range(rows // block):
            at = r * block
            mask = (band & ((key >= WINDOW) | present)) if r == 0 else band
            s = jnp.where(mask, products[r], -1e30)
            p = jnp.exp2((s - jnp.max(s, axis=0, keepdims=True)) * scale)
            wsum = jnp.sum(p, axis=0, keepdims=True)
            wnum = mm(vt[:, at : at + span], p.astype(BF))
            for k in range(2):
                mine = slice(k * block, (k + 1) * block)
                mixed = k * (rows // wide) + at // wide
                part = slice(at % wide, at % wide + block)
                num_ref[out + pair + k, :, at : at + block] = (
                    mixes[k] * wnum[:, mine] + rests[k] * lnums[mixed][:, part]
                )
                den_ref[out + pair + k, :, at : at + block] = (
                    mixes[k] * wsum[:, mine] + rests[k] * lsums[mixed][:, part]
                )


def finished(per_part, which, half, first, idx_ref, share_ref, held, pieces):
    at = pl.ds(pl.multiple_of(idx_ref[which] * half, 128), half)
    slot = 0
    for num, den, qf in held:
        count, width, _ = num.shape
        for n in range(count):
            m, e = divmod(slot, per_part)
            slot += 1
            if not first <= m < first + len(pieces):
                continue
            head = lax.bitwise_xor(idx_ref[0], m) * per_part + e
            rest = 1.0 - jax.nn.sigmoid(jnp.full((1, half), share_ref[head], F32))
            both = mm(pieces[m - first][e], qf[n, :, at])
            numer = num[n, :, at] + rest * both[:width]
            denom = den[n, :, at] + rest * (both[width : width + 1] + both[width + 1 : width + 2])
            yield m, e, (numer * (1.0 / denom)).astype(BF).T


def quarter_at(core, m, per_part, idx_ref):
    return pl.ds((idx_ref[core] * PART + lax.bitwise_xor(idx_ref[0], m)) * per_part, per_part)


def final_own_kernel(per_part, half, idx_ref, share_ref, num, den, qf, piece, sent_ref, kept):
    held, pieces = [(num, den, qf)], [piece]
    for _, e, rows in finished(per_part, 3, half, 0, idx_ref, share_ref, held, pieces):
        sent_ref[e] = rows
    for _, e, rows in finished(per_part, 2, half, 0, idx_ref, share_ref, held, pieces):
        kept[e] = rows


def final_sent_kernel(per_part, half, idx_ref, share_ref, *refs):
    held, pieces, out_ref = (refs[:3], refs[3:6]), refs[6 : 5 + PART], refs[-1]
    for m, e, rows in finished(per_part, 3, half, 1, idx_ref, share_ref, held, pieces):
        out_ref[(m - 1) * per_part + e] = rows


def final_kept_kernel(per_part, half, idx_ref, share_ref, *refs):
    held, pieces = (refs[:3], refs[3:6]), refs[6 : 5 + PART]
    out_ref, kept, sems = refs[-3:]
    copies = [pltpu.make_async_copy(refs[5 + PART], out_ref.at[quarter_at(2, 0, per_part, idx_ref)], sems.at[0])]
    copies[0].start()
    for m, e, rows in finished(per_part, 2, half, 1, idx_ref, share_ref, held, pieces):
        kept[m - 1, e] = rows
        if e == per_part - 1:
            copies.append(
                pltpu.make_async_copy(kept.at[m - 1], out_ref.at[quarter_at(2, m, per_part, idx_ref)], sems.at[m])
            )
            copies[-1].start()
    for copy in copies:
        copy.wait()


def place_kernel(per_part, idx_ref, own_ref, got_ref, _, out_ref, sems):
    copies = [
        pltpu.make_async_copy(
            got_ref.at[pl.ds((m - 1) * per_part, per_part)] if m else own_ref,
            out_ref.at[quarter_at(3, m, per_part, idx_ref)],
            sems.at[m],
        )
        for m in range(PART)
    ]
    for copy in copies:
        copy.start()
    for copy in copies:
        copy.wait()


def per_device(queries, key_vectors, value_vectors, query_map, key_map, window_param):
    rows, heads, width = queries.shape
    groups = key_vectors.shape[1]
    group_size = heads // groups
    feat = query_map.shape[2]
    per_part = heads // PART
    tall = width + 8
    devices = lax.axis_size("seq")
    zs = devices // PART
    position = lax.axis_index("seq")
    core = lax.axis_index("head")
    me = position % PART
    idx = jnp.stack([me, position, core, 1 - core]).astype(jnp.int32)
    params = pltpu.CompilerParams(vmem_limit_bytes=LIMIT)
    smem = pl.BlockSpec(memory_space=pltpu.SMEM)
    anywhere = pl.BlockSpec(memory_space=pl.ANY)
    vmem = pl.BlockSpec(memory_space=pltpu.VMEM)
    query_map = query_map.transpose(0, 2, 1)
    key_map = key_map.transpose(0, 2, 1)

    def xor(x, m):
        return lax.ppermute(x, "seq", [(i, i ^ m) for i in range(devices)])

    def shift(x, by):
        return lax.ppermute(x, "seq", [(i, i + by) for i in range(devices - by)])

    piece_shape = jax.ShapeDtypeStruct((per_part, tall, width), BF)
    grouped = jax.ShapeDtypeStruct((groups, rows, width), BF)
    feat_shape = jax.ShapeDtypeStruct((heads, rows, width), BF)
    hbm = pl.BlockSpec(memory_space=pltpu.HBM)
    own_feat, keys, values, values_t, *pieces = pl.pallas_call(
        functools.partial(sent_states_kernel, per_part, group_size),
        in_specs=[smem] + [hbm] * 3,
        out_specs=[vmem] * (4 + PART - 1),
        out_shape=[
            feat_shape,
            grouped,
            grouped,
            jax.ShapeDtypeStruct((groups, tall, rows), BF),
        ]
        + [piece_shape] * (PART - 1),
        scratch_shapes=[
            pltpu.VMEM((rows, groups, width), BF),
            pltpu.VMEM((rows, groups, width), BF),
            pltpu.VMEM(key_map.shape, BF),
            pltpu.SemaphoreType.DMA((3,)),
        ],
        compiler_params=params,
        name="sent_states",
    )(idx, *(pltpu.with_memory_space_constraint(x, pltpu.HBM) for x in (key_vectors, value_vectors, key_map)))
    pieces = [xor(pieces[m - 1], m) for m in range(1, PART)]
    own_feat, own_piece, tails = pl.pallas_call(
        functools.partial(own_states_kernel, per_part, group_size),
        in_specs=[smem] + [vmem] * 5,
        out_specs=[vmem] * 3,
        out_shape=[feat_shape, piece_shape, jax.ShapeDtypeStruct((2, groups, WINDOW, width), BF)],
        input_output_aliases={5: 0},
        compiler_params=params,
        cost_estimate=pl.CostEstimate(flops=10**9, bytes_accessed=2 * 10**6, transcendentals=10**6),
        name="own_states",
    )(idx, keys, values, values_t, key_map, own_feat)
    halo = shift(tails, 1)
    pieces = [own_piece] + pieces
    total = pl.pallas_call(
        total_kernel, in_specs=[vmem] * PART, out_specs=vmem, out_shape=piece_shape, compiler_params=params, name="totals"
    )(*pieces)
    exchanged = zs in (1, 2, 4)
    if exchanged:
        earlier = [xor(total, PART * k) for k in range(1, zs)]
    else:
        columns = [[z * PART + k for z in range(zs)] for k in range(PART)]
        gathered = lax.all_gather(total, "seq", axis_index_groups=columns)
        below = jnp.arange(zs) < position // PART
        summed = jnp.sum(jnp.where(below[:, None, None, None], gathered.astype(F32), 0.0), axis=0)
        high = summed.astype(BF)
        earlier = [high, (summed - high.astype(F32)).astype(BF)]
    q_wide, keys, values = pl.pallas_call(
        functools.partial(prepare_kernel, group_size),
        in_specs=[vmem] * 4 + [anywhere],
        out_specs=[vmem] * 3,
        out_shape=[
            jax.ShapeDtypeStruct((groups, rows * group_size, width), F32),
            jax.ShapeDtypeStruct((groups, WINDOW + rows, width), BF),
            jax.ShapeDtypeStruct((groups, width, WINDOW + rows), BF),
        ],
        compiler_params=params,
        name="prepare",
    )(queries, keys, values, halo, total)

    def near(first, count, after):
        return pl.pallas_call(
            functools.partial(near_kernel, group_size, per_part, first, STEP),
            grid=(count // STEP,),
            in_specs=[smem, smem] + [vmem] * 6 + [anywhere] * len(after),
            out_specs=[vmem] * 3,
            scratch_shapes=[pltpu.VMEM((STEP, WINDOW + rows, 2 * feat), BF)],
            out_shape=[
                jax.ShapeDtypeStruct((count, width, rows), F32),
                jax.ShapeDtypeStruct((count, 1, rows), F32),
                jax.ShapeDtypeStruct((count, 2 * feat, rows), BF),
            ],
            compiler_params=params,
            cost_estimate=pl.CostEstimate(
                flops=count * 4 * 10**8, bytes_accessed=count * 10**6, transcendentals=count * 3 * 10**5
            ),
            name="near_%d" % first,
        )(idx, window_param, q_wide, keys, values, own_feat, query_map, key_map, *after)

    held = list(near(0, SPLIT, []))
    prefixes = pl.pallas_call(
        functools.partial(prefix_kernel, len(earlier), exchanged),
        in_specs=[smem] + [vmem] * (PART + len(earlier)) + [anywhere],
        out_specs=[vmem] * PART,
        out_shape=[piece_shape] * PART,
        compiler_params=params,
        name="prefixes",
    )(idx, *pieces, *earlier, held[1])
    prior = [prefixes[0]] + [xor(prefixes[m], m) for m in range(1, PART)]
    held += near(SPLIT, heads - SPLIT, [prefixes[0]])

    half = rows // 2
    out_shape = jax.ShapeDtypeStruct((2 * heads, half, width), BF)

    def swapped(x):
        return lax.ppermute(x, "head", [(0, 1), (1, 0)])

    sent_own, kept_own = pl.pallas_call(
        functools.partial(final_own_kernel, per_part, half),
        in_specs=[smem, smem] + [vmem] * 4,
        out_specs=[vmem] * 2,
        out_shape=[jax.ShapeDtypeStruct((per_part, half, width), BF)] * 2,
        compiler_params=params,
        cost_estimate=pl.CostEstimate(flops=5 * 10**8, bytes_accessed=2 * 10**6, transcendentals=0),
        name="final_own",
    )(idx, window_param, *held[:3], prior[0])
    got_own = swapped(sent_own)
    sent = pl.pallas_call(
        functools.partial(final_sent_kernel, per_part, half),
        in_specs=[smem, smem] + [vmem] * (5 + PART) + [anywhere],
        out_specs=vmem,
        out_shape=jax.ShapeDtypeStruct((heads - per_part, half, width), BF),
        compiler_params=params,
        name="final_sent",
    )(idx, window_param, *held, *prior[1:], sent_own)
    got = swapped(sent)
    out = pl.pallas_call(
        functools.partial(final_kept_kernel, per_part, half),
        in_specs=[smem, smem] + [vmem] * (6 + PART) + [anywhere],
        out_specs=hbm,
        out_shape=out_shape,
        scratch_shapes=[pltpu.VMEM((PART - 1, per_part, half, width), BF), pltpu.SemaphoreType.DMA((PART,))],
        compiler_params=params,
        cost_estimate=pl.CostEstimate(flops=10**9, bytes_accessed=5 * 10**6, transcendentals=0),
        name="final_kept",
    )(idx, window_param, *held, *prior[1:], kept_own, sent)
    return pl.pallas_call(
        functools.partial(place_kernel, per_part),
        in_specs=[smem, vmem, vmem, hbm],
        out_specs=hbm,
        out_shape=out_shape,
        scratch_shapes=[pltpu.SemaphoreType.DMA((PART,))],
        input_output_aliases={3: 0},
        compiler_params=params,
        name="place",
    )(idx, got_own, got, out)


def solution(mesh):
    in_specs = (
        P("seq", "head", None),
        P("seq", "head", None),
        P("seq", "head", None),
        P("head", None, None),
        P("head", None, None),
        P("head"),
    )
    out_specs = P(None, ("seq", "head"), None)
    return jax.shard_map(
        per_device, mesh=mesh, in_specs=in_specs, out_specs=out_specs, check_vma=False
    )
```

```python
import functools

import jax
import jax.numpy as jnp
import numpy as np
from jax import lax
from jax.experimental import pallas as pl
from jax.experimental.pallas import tpu as pltpu
from jax.sharding import PartitionSpec as P

WINDOW = 64
PART = 4
BF = jnp.bfloat16
F32 = jnp.float32
LIMIT = 16 * 1024 * 1024
STEP = 4
SPLIT = 12


def mm(a, b, ca=1, cb=0):
    return lax.dot_general(a, b, (((ca,), (cb,)), ((), ())), preferred_element_type=F32)


def features_t(logits):
    top = jnp.max(logits, axis=0, keepdims=True)
    low = jnp.min(logits, axis=0, keepdims=True)
    up = jnp.exp(logits - top)
    down = jnp.exp(low - logits)
    up = up * (1.0 / jnp.sum(up, axis=0, keepdims=True))
    down = down * (1.0 / jnp.sum(down, axis=0, keepdims=True))
    return jnp.concatenate([up, down], axis=0).astype(BF)


def put_state(ref, e, state, norm):
    width = state.shape[-1]
    high = norm.astype(BF).astype(F32)
    row = lax.broadcasted_iota(jnp.int32, (8, width), 0)
    ref[e, :width] = state.astype(BF)
    ref[e, width:] = jnp.where(row == 0, high, jnp.where(row == 1, norm - high, 0.0)).astype(BF)


def get_state(ref, e):
    width = ref.shape[-1]
    last = ref[e, width:].astype(F32)
    return ref[e, :width].astype(F32), last[0:1] + last[1:2]


def values_with_one(values):
    row = lax.broadcasted_iota(jnp.int32, (8, values.shape[0]), 0)
    return jnp.concatenate([values.T, jnp.where(row == 0, 1.0, 0.0).astype(BF)], axis=0)


def quarter_states(m, per_part, group_size, idx_ref, k_ref, vt_ref, w_ref, feat_ref, out):
    head = lax.bitwise_xor(idx_ref[0], m) * per_part
    g = head // group_size
    logits = mm(w_ref[pl.ds(head, per_part)].reshape(-1, k_ref.shape[-1]), k_ref[g], 1, 1)
    f = w_ref.shape[1]
    for e in range(per_part):
        feat = features_t(logits[e * f : (e + 1) * f]).T
        feat_ref[head + e] = feat
        state = mm(vt_ref[g], feat)
        width = state.shape[-1]
        put_state(out, e, state[:width], state[width : width + 1])


def sent_states_kernel(
    per_part, group_size, idx_ref, k_hbm, v_hbm, w_hbm, feat_ref, kg_ref, vg_ref, vt_ref, w_raw, p1, p2, p3,
    k_raw, v_raw, sems,
):
    rows, groups, _ = k_raw.shape
    copies = []
    for source, target in ((k_hbm, k_raw), (w_hbm, w_raw), (v_hbm, v_raw)):
        part = source.shape[0] // 2
        for n in range(2):
            at = pl.ds(n * part, part)
            copies.append(pltpu.make_async_copy(source.at[at], target.at[at], sems.at[len(copies)]))
            copies[-1].start()
    for copy in copies[:2]:
        copy.wait()
    wide = k_raw[...].astype(F32)
    for g in range(groups):
        kg_ref[g] = wide[:, g].astype(BF)
    for copy in copies[2:]:
        copy.wait()
    wide = v_raw[...].astype(F32)
    for g in range(groups):
        values = wide[:, g].astype(BF)
        vg_ref[g] = values
        vt_ref[g] = values_with_one(values)
    for m, out in enumerate((p1, p2, p3), 1):
        quarter_states(m, per_part, group_size, idx_ref, kg_ref, vt_ref, w_raw, feat_ref, out)


def own_states_kernel(per_part, group_size, idx_ref, k_ref, v_ref, vt_ref, w_ref, _, feat_ref, out, tail_ref):
    rows = k_ref.shape[1]
    tail_ref[0] = k_ref[:, rows - WINDOW :]
    tail_ref[1] = v_ref[:, rows - WINDOW :]
    quarter_states(0, per_part, group_size, idx_ref, k_ref, vt_ref, w_ref, feat_ref, out)


def total_kernel(a, b, c, d, out):
    for e in range(out.shape[0]):
        states, norms = zip(*(get_state(ref, e) for ref in (a, b, c, d)))
        put_state(out, e, sum(states[1:], states[0]), sum(norms[1:], norms[0]))


def prefix_kernel(zs, exchanged, idx_ref, *refs):
    layer = idx_ref[1] // PART
    own, later, outs = refs[:PART], refs[PART : PART + zs], refs[PART + zs + 1 :]
    me = idx_ref[0]
    for e in range(outs[0].shape[0]):
        base = None
        for k, ref in enumerate(later, 1):
            term = get_state(ref, e)
            if exchanged:
                term = tuple(jnp.where(lax.bitwise_xor(layer, k) < layer, x, 0.0) for x in term)
            base = term if base is None else (base[0] + term[0], base[1] + term[1])
        terms = [get_state(ref, e) for ref in own]
        for m in range(PART):
            total = base
            for k in range(PART):
                if k != m:
                    earlier = lax.bitwise_xor(me, k) < lax.bitwise_xor(me, m)
                    total = tuple(t + jnp.where(earlier, x, 0.0) for t, x in zip(total, terms[k]))
            put_state(outs[m], e, *total)


def prepare_kernel(group_size, q_ref, k_ref, v_ref, halo_ref, _, q_wide, kx, vt):
    rows, _, width = q_ref.shape
    for g in range(k_ref.shape[0]):
        q = q_ref[:, g * group_size : (g + 1) * group_size].astype(F32)
        q_wide[g] = q.reshape(rows * group_size, width)
        kx[g, :WINDOW] = halo_ref[0, g]
        kx[g, WINDOW:] = k_ref[g]
        vt[g] = jnp.concatenate([halo_ref[1, g], v_ref[g]], axis=0).T


def near_kernel(group_size, per_part, first, count, idx_ref, share_ref, q_wide, kx_ref, vt_ref, feat_ref, wq_ref, wk_ref, *refs):
    num_ref, den_ref, qf_ref, fx = refs[-4:]
    out = pl.program_id(0) * count
    slot = first + out
    head = lax.bitwise_xor(idx_ref[0], slot // per_part) * per_part + slot % per_part
    g = head // group_size
    rows, width = feat_ref.shape[1:]
    scale = np.float32(np.log2(np.e) / np.sqrt(width))
    kx, vt = kx_ref.at[g], vt_ref.at[g]
    present = idx_ref[1] > 0
    block = 128
    span = block + WINDOW
    key = lax.broadcasted_iota(jnp.int32, (span, 2 * block), 0)
    row = lax.broadcasted_iota(jnp.int32, (span, 2 * block), 1) % block
    band = (key > row) & (key <= row + WINDOW)
    wide = 2 * block
    causal = lax.broadcasted_iota(jnp.int32, (wide, wide), 0) <= lax.broadcasted_iota(jnp.int32, (wide, wide), 1)
    halo_logits = mm(wk_ref[pl.ds(head, count)].reshape(-1, width), kx[:128], 1, 1)
    feat = halo_logits.shape[0] // count
    for pair in range(0, count, 2):
        qs, mixes, rests, lnums, lsums = [], [], [], [], []
        products, logits = [], [[], []]
        for r in range(rows // block):
            at = r * block
            both = jnp.concatenate(
                [
                    q_wide[g, pl.ds(at * group_size + head % group_size + e, block, stride=group_size), :].astype(BF)
                    for e in (pair, pair + 1)
                ],
                axis=0,
            )
            maps = [wq_ref[head + pair], wq_ref[head + pair + 1], kx[at : at + span]]
            x = mm(jnp.concatenate(maps, axis=0), both, 1, 1)
            logits[0].append(x[:feat, :block])
            logits[1].append(x[feat : 2 * feat, block:])
            products.append(x[2 * feat :])
        for e in (pair, pair + 1):
            halo_feat = features_t(halo_logits[e * feat : (e + 1) * feat]).T[:WINDOW]
            fx[e, :WINDOW] = jnp.where(present, halo_feat.astype(F32), 0.0).astype(BF)
            fx[e, WINDOW:] = feat_ref[head + e]
            mixes.append(jax.nn.sigmoid(jnp.full((1, block), share_ref[head + e], F32)))
            rests.append(1.0 - mixes[-1])
            qf = features_t(jnp.concatenate(logits[e - pair], axis=1))
            qf_ref[out + e] = qf
            for r in range(rows // wide):
                at = r * wide
                lnum = None
                lsum = None
                for kc in range(r + 1):
                    a = mm(fx[e, kc * wide : kc * wide + wide], qf[:, at : at + wide])
                    if kc == r:
                        last = jnp.where(causal, a, 0.0)
                    else:
                        last = a
                    if kc == 0:
                        halo = a[:WINDOW]
                        kept = halo.astype(BF).astype(F32)
                        body = last[WINDOW:]
                        part = jnp.sum(body, axis=0, keepdims=True)
                        if r == 0:
                            inside = causal[:WINDOW]
                            kept = jnp.where(inside, kept, 0.0)
                            part = part - jnp.sum(jnp.where(inside, 0.0, halo), axis=0, keepdims=True)
                        w = jnp.concatenate([(kept - halo).astype(BF), body.astype(BF)], axis=0)
                    else:
                        w = last.astype(BF)
                        part = jnp.sum(last, axis=0, keepdims=True)
                    t = mm(vt[:, kc * wide : kc * wide + wide], w)
                    lnum = t if lnum is None else lnum + t
                    lsum = part if lsum is None else lsum + part
                lnums.append(lnum)
                lsums.append(lsum)
        for r in range(rows // block):
            at = r * block
            mask = (band & ((key >= WINDOW) | present)) if r == 0 else band
            s = jnp.where(mask, products[r], -1e30)
            p = jnp.exp2((s - jnp.max(s, axis=0, keepdims=True)) * scale)
            wsum = jnp.sum(p, axis=0, keepdims=True)
            wnum = mm(vt[:, at : at + span], p.astype(BF))
            for k in range(2):
                mine = slice(k * block, (k + 1) * block)
                mixed = k * (rows // wide) + at // wide
                part = slice(at % wide, at % wide + block)
                num_ref[out + pair + k, :, at : at + block] = (
                    mixes[k] * wnum[:, mine] + rests[k] * lnums[mixed][:, part]
                )
                den_ref[out + pair + k, :, at : at + block] = (
                    mixes[k] * wsum[:, mine] + rests[k] * lsums[mixed][:, part]
                )


def finished(per_part, which, half, first, idx_ref, share_ref, held, pieces):
    at = pl.ds(pl.multiple_of(idx_ref[which] * half, 128), half)
    slot = 0
    for num, den, qf in held:
        count, width, _ = num.shape
        for n in range(count):
            m, e = divmod(slot, per_part)
            slot += 1
            if not first <= m < first + len(pieces):
                continue
            head = lax.bitwise_xor(idx_ref[0], m) * per_part + e
            rest = 1.0 - jax.nn.sigmoid(jnp.full((1, half), share_ref[head], F32))
            both = mm(pieces[m - first][e], qf[n, :, at])
            numer = num[n, :, at] + rest * both[:width]
            denom = den[n, :, at] + rest * (both[width : width + 1] + both[width + 1 : width + 2])
            yield m, e, (numer * (1.0 / denom)).astype(BF).T


def quarter_at(core, m, per_part, idx_ref):
    return pl.ds((idx_ref[core] * PART + lax.bitwise_xor(idx_ref[0], m)) * per_part, per_part)


def final_own_kernel(per_part, half, idx_ref, share_ref, num, den, qf, piece, sent_ref, kept):
    held, pieces = [(num, den, qf)], [piece]
    for _, e, rows in finished(per_part, 3, half, 0, idx_ref, share_ref, held, pieces):
        sent_ref[e] = rows
    for _, e, rows in finished(per_part, 2, half, 0, idx_ref, share_ref, held, pieces):
        kept[e] = rows


def final_sent_kernel(per_part, half, idx_ref, share_ref, *refs):
    held, pieces, out_ref = (refs[:3], refs[3:6]), refs[6 : 5 + PART], refs[-1]
    for m, e, rows in finished(per_part, 3, half, 1, idx_ref, share_ref, held, pieces):
        out_ref[(m - 1) * per_part + e] = rows


def final_kept_kernel(per_part, half, idx_ref, share_ref, *refs):
    held, pieces = (refs[:3], refs[3:6]), refs[6 : 5 + PART]
    out_ref, kept, sems = refs[-3:]
    copies = [pltpu.make_async_copy(refs[5 + PART], out_ref.at[quarter_at(2, 0, per_part, idx_ref)], sems.at[0])]
    copies[0].start()
    for m, e, rows in finished(per_part, 2, half, 1, idx_ref, share_ref, held, pieces):
        kept[m - 1, e] = rows
        if e == per_part - 1:
            copies.append(
                pltpu.make_async_copy(kept.at[m - 1], out_ref.at[quarter_at(2, m, per_part, idx_ref)], sems.at[m])
            )
            copies[-1].start()
    for copy in copies:
        copy.wait()


def place_kernel(per_part, idx_ref, own_ref, got_ref, _, out_ref, sems):
    copies = [
        pltpu.make_async_copy(
            got_ref.at[pl.ds((m - 1) * per_part, per_part)] if m else own_ref,
            out_ref.at[quarter_at(3, m, per_part, idx_ref)],
            sems.at[m],
        )
        for m in range(PART)
    ]
    for copy in copies:
        copy.start()
    for copy in copies:
        copy.wait()


def per_device(queries, key_vectors, value_vectors, query_map, key_map, window_param):
    rows, heads, width = queries.shape
    groups = key_vectors.shape[1]
    group_size = heads // groups
    feat = query_map.shape[2]
    per_part = heads // PART
    tall = width + 8
    devices = lax.axis_size("seq")
    zs = devices // PART
    position = lax.axis_index("seq")
    core = lax.axis_index("head")
    me = position % PART
    idx = jnp.stack([me, position, core, 1 - core]).astype(jnp.int32)
    params = pltpu.CompilerParams(vmem_limit_bytes=LIMIT)
    smem = pl.BlockSpec(memory_space=pltpu.SMEM)
    anywhere = pl.BlockSpec(memory_space=pl.ANY)
    vmem = pl.BlockSpec(memory_space=pltpu.VMEM)
    query_map = query_map.transpose(0, 2, 1)
    key_map = key_map.transpose(0, 2, 1)

    def xor(x, m):
        return lax.ppermute(x, "seq", [(i, i ^ m) for i in range(devices)])

    def shift(x, by):
        return lax.ppermute(x, "seq", [(i, i + by) for i in range(devices - by)])

    piece_shape = jax.ShapeDtypeStruct((per_part, tall, width), BF)
    grouped = jax.ShapeDtypeStruct((groups, rows, width), BF)
    feat_shape = jax.ShapeDtypeStruct((heads, rows, width), BF)
    hbm = pl.BlockSpec(memory_space=pltpu.HBM)
    own_feat, keys, values, values_t, key_map, *pieces = pl.pallas_call(
        functools.partial(sent_states_kernel, per_part, group_size),
        in_specs=[smem] + [hbm] * 3,
        out_specs=[vmem] * (5 + PART - 1),
        out_shape=[
            feat_shape,
            grouped,
            grouped,
            jax.ShapeDtypeStruct((groups, tall, rows), BF),
            jax.ShapeDtypeStruct(key_map.shape, BF),
        ]
        + [piece_shape] * (PART - 1),
        scratch_shapes=[
            pltpu.VMEM((rows, groups, width), BF),
            pltpu.VMEM((rows, groups, width), BF),
            pltpu.SemaphoreType.DMA((6,)),
        ],
        compiler_params=params,
        name="sent_states",
    )(idx, *(pltpu.with_memory_space_constraint(x, pltpu.HBM) for x in (key_vectors, value_vectors, key_map)))
    pieces = [xor(pieces[m - 1], m) for m in range(1, PART)]
    own_feat, own_piece, tails = pl.pallas_call(
        functools.partial(own_states_kernel, per_part, group_size),
        in_specs=[smem] + [vmem] * 5,
        out_specs=[vmem] * 3,
        out_shape=[feat_shape, piece_shape, jax.ShapeDtypeStruct((2, groups, WINDOW, width), BF)],
        input_output_aliases={5: 0},
        compiler_params=params,
        cost_estimate=pl.CostEstimate(flops=10**9, bytes_accessed=2 * 10**6, transcendentals=10**6),
        name="own_states",
    )(idx, keys, values, values_t, key_map, own_feat)
    halo = shift(tails, 1)
    pieces = [own_piece] + pieces
    total = pl.pallas_call(
        total_kernel, in_specs=[vmem] * PART, out_specs=vmem, out_shape=piece_shape, compiler_params=params, name="totals"
    )(*pieces)
    exchanged = zs in (1, 2, 4)
    if exchanged:
        earlier = [xor(total, PART * k) for k in range(1, zs)]
    else:
        columns = [[z * PART + k for z in range(zs)] for k in range(PART)]
        gathered = lax.all_gather(total, "seq", axis_index_groups=columns)
        below = jnp.arange(zs) < position // PART
        summed = jnp.sum(jnp.where(below[:, None, None, None], gathered.astype(F32), 0.0), axis=0)
        high = summed.astype(BF)
        earlier = [high, (summed - high.astype(F32)).astype(BF)]
    q_wide, keys, values = pl.pallas_call(
        functools.partial(prepare_kernel, group_size),
        in_specs=[vmem] * 4 + [anywhere],
        out_specs=[vmem] * 3,
        out_shape=[
            jax.ShapeDtypeStruct((groups, rows * group_size, width), F32),
            jax.ShapeDtypeStruct((groups, WINDOW + rows, width), BF),
            jax.ShapeDtypeStruct((groups, width, WINDOW + rows), BF),
        ],
        compiler_params=params,
        name="prepare",
    )(queries, keys, values, halo, total)

    def near(first, count, after):
        return pl.pallas_call(
            functools.partial(near_kernel, group_size, per_part, first, STEP),
            grid=(count // STEP,),
            in_specs=[smem, smem] + [vmem] * 6 + [anywhere] * len(after),
            out_specs=[vmem] * 3,
            scratch_shapes=[pltpu.VMEM((STEP, WINDOW + rows, 2 * feat), BF)],
            out_shape=[
                jax.ShapeDtypeStruct((count, width, rows), F32),
                jax.ShapeDtypeStruct((count, 1, rows), F32),
                jax.ShapeDtypeStruct((count, 2 * feat, rows), BF),
            ],
            compiler_params=params,
            cost_estimate=pl.CostEstimate(
                flops=count * 4 * 10**8, bytes_accessed=count * 10**6, transcendentals=count * 3 * 10**5
            ),
            name="near_%d" % first,
        )(idx, window_param, q_wide, keys, values, own_feat, query_map, key_map, *after)

    held = list(near(0, SPLIT, []))
    prefixes = pl.pallas_call(
        functools.partial(prefix_kernel, len(earlier), exchanged),
        in_specs=[smem] + [vmem] * (PART + len(earlier)) + [anywhere],
        out_specs=[vmem] * PART,
        out_shape=[piece_shape] * PART,
        compiler_params=params,
        name="prefixes",
    )(idx, *pieces, *earlier, held[1])
    prior = [prefixes[0]] + [xor(prefixes[m], m) for m in range(1, PART)]
    held += near(SPLIT, heads - SPLIT, [prefixes[0]])

    half = rows // 2
    out_shape = jax.ShapeDtypeStruct((2 * heads, half, width), BF)

    def swapped(x):
        return lax.ppermute(x, "head", [(0, 1), (1, 0)])

    sent_own, kept_own = pl.pallas_call(
        functools.partial(final_own_kernel, per_part, half),
        in_specs=[smem, smem] + [vmem] * 4,
        out_specs=[vmem] * 2,
        out_shape=[jax.ShapeDtypeStruct((per_part, half, width), BF)] * 2,
        compiler_params=params,
        cost_estimate=pl.CostEstimate(flops=5 * 10**8, bytes_accessed=2 * 10**6, transcendentals=0),
        name="final_own",
    )(idx, window_param, *held[:3], prior[0])
    got_own = swapped(sent_own)
    sent = pl.pallas_call(
        functools.partial(final_sent_kernel, per_part, half),
        in_specs=[smem, smem] + [vmem] * (5 + PART) + [anywhere],
        out_specs=vmem,
        out_shape=jax.ShapeDtypeStruct((heads - per_part, half, width), BF),
        compiler_params=params,
        name="final_sent",
    )(idx, window_param, *held, *prior[1:], sent_own)
    got = swapped(sent)
    out = pl.pallas_call(
        functools.partial(final_kept_kernel, per_part, half),
        in_specs=[smem, smem] + [vmem] * (6 + PART) + [anywhere],
        out_specs=hbm,
        out_shape=out_shape,
        scratch_shapes=[pltpu.VMEM((PART - 1, per_part, half, width), BF), pltpu.SemaphoreType.DMA((PART,))],
        compiler_params=params,
        cost_estimate=pl.CostEstimate(flops=10**9, bytes_accessed=5 * 10**6, transcendentals=0),
        name="final_kept",
    )(idx, window_param, *held, *prior[1:], kept_own, sent)
    return pl.pallas_call(
        functools.partial(place_kernel, per_part),
        in_specs=[smem, vmem, vmem, hbm],
        out_specs=hbm,
        out_shape=out_shape,
        scratch_shapes=[pltpu.SemaphoreType.DMA((PART,))],
        input_output_aliases={3: 0},
        compiler_params=params,
        name="place",
    )(idx, got_own, got, out)


def solution(mesh):
    in_specs = (
        P("seq", "head", None),
        P("seq", "head", None),
        P("seq", "head", None),
        P("head", None, None),
        P("head", None, None),
        P("head"),
    )
    out_specs = P(None, ("seq", "head"), None)
    return jax.shard_map(
        per_device, mesh=mesh, in_specs=in_specs, out_specs=out_specs, check_vma=False
    )
```

```python
import functools

import jax
import jax.numpy as jnp
import numpy as np
from jax import lax
from jax.experimental import pallas as pl
from jax.experimental.pallas import tpu as pltpu
from jax.sharding import PartitionSpec as P

WINDOW = 64
PART = 4
BF = jnp.bfloat16
F32 = jnp.float32
LIMIT = 16 * 1024 * 1024
STEP = 4
SPLIT = (4, 12)


def mm(a, b, ca=1, cb=0):
    return lax.dot_general(a, b, (((ca,), (cb,)), ((), ())), preferred_element_type=F32)


def features_t(logits):
    top = jnp.max(logits, axis=0, keepdims=True)
    low = jnp.min(logits, axis=0, keepdims=True)
    up = jnp.exp(logits - top)
    down = jnp.exp(low - logits)
    up = up * (1.0 / jnp.sum(up, axis=0, keepdims=True))
    down = down * (1.0 / jnp.sum(down, axis=0, keepdims=True))
    return jnp.concatenate([up, down], axis=0).astype(BF)


def put_state(ref, e, state, norm):
    width = state.shape[-1]
    high = norm.astype(BF).astype(F32)
    row = lax.broadcasted_iota(jnp.int32, (8, width), 0)
    ref[e, :width] = state.astype(BF)
    ref[e, width:] = jnp.where(row == 0, high, jnp.where(row == 1, norm - high, 0.0)).astype(BF)


def get_state(ref, e):
    width = ref.shape[-1]
    last = ref[e, width:].astype(F32)
    return ref[e, :width].astype(F32), last[0:1] + last[1:2]


def values_with_one(values):
    row = lax.broadcasted_iota(jnp.int32, (8, values.shape[0]), 0)
    return jnp.concatenate([values.T, jnp.where(row == 0, 1.0, 0.0).astype(BF)], axis=0)


def quarter_states(m, per_part, group_size, idx_ref, k_ref, vt_ref, w_ref, feat_ref, out):
    head = lax.bitwise_xor(idx_ref[0], m) * per_part
    g = head // group_size
    logits = mm(w_ref[pl.ds(head, per_part)].reshape(-1, k_ref.shape[-1]), k_ref[g], 1, 1)
    f = w_ref.shape[1]
    for e in range(per_part):
        feat = features_t(logits[e * f : (e + 1) * f]).T
        feat_ref[head + e] = feat
        state = mm(vt_ref[g], feat)
        width = state.shape[-1]
        put_state(out, e, state[:width], state[width : width + 1])


def sent_states_kernel(
    per_part, group_size, idx_ref, k_hbm, v_hbm, w_hbm, feat_ref, kg_ref, vg_ref, vt_ref, w_raw, p1, p2, p3,
    k_raw, v_raw, sems,
):
    rows, groups, _ = k_raw.shape
    copies = []
    for source, target in ((k_hbm, k_raw), (w_hbm, w_raw), (v_hbm, v_raw)):
        part = source.shape[0] // 2
        for n in range(2):
            at = pl.ds(n * part, part)
            copies.append(pltpu.make_async_copy(source.at[at], target.at[at], sems.at[len(copies)]))
            copies[-1].start()
    for copy in copies[:2]:
        copy.wait()
    wide = k_raw[...].astype(F32)
    for g in range(groups):
        kg_ref[g] = wide[:, g].astype(BF)
    for copy in copies[2:]:
        copy.wait()
    wide = v_raw[...].astype(F32)
    for g in range(groups):
        values = wide[:, g].astype(BF)
        vg_ref[g] = values
        vt_ref[g] = values_with_one(values)
    for m, out in enumerate((p1, p2, p3), 1):
        quarter_states(m, per_part, group_size, idx_ref, kg_ref, vt_ref, w_raw, feat_ref, out)


def own_states_kernel(per_part, group_size, idx_ref, k_ref, v_ref, vt_ref, w_ref, _, feat_ref, out, tail_ref):
    rows = k_ref.shape[1]
    tail_ref[0] = k_ref[:, rows - WINDOW :]
    tail_ref[1] = v_ref[:, rows - WINDOW :]
    quarter_states(0, per_part, group_size, idx_ref, k_ref, vt_ref, w_ref, feat_ref, out)


def total_kernel(a, b, c, d, out):
    for e in range(out.shape[0]):
        states, norms = zip(*(get_state(ref, e) for ref in (a, b, c, d)))
        put_state(out, e, sum(states[1:], states[0]), sum(norms[1:], norms[0]))


def sum_kernel(a, b, _, out):
    for e in range(out.shape[0]):
        state, norm = zip(get_state(a, e), get_state(b, e))
        put_state(out, e, state[0] + state[1], norm[0] + norm[1])


def prefix_kernel(zs, exchanged, idx_ref, *refs):
    layer = idx_ref[1] // PART
    own, later, outs = refs[:PART], refs[PART : PART + zs], refs[PART + zs + 1 :]
    me = idx_ref[0]
    for e in range(outs[0].shape[0]):
        base = None
        for k, ref in enumerate(later, 1):
            term = get_state(ref, e)
            if exchanged:
                term = tuple(jnp.where(lax.bitwise_xor(layer, k) < layer, x, 0.0) for x in term)
            base = term if base is None else (base[0] + term[0], base[1] + term[1])
        terms = [get_state(ref, e) for ref in own]
        for m in range(PART):
            total = base
            for k in range(PART):
                if k != m:
                    earlier = lax.bitwise_xor(me, k) < lax.bitwise_xor(me, m)
                    total = tuple(t + jnp.where(earlier, x, 0.0) for t, x in zip(total, terms[k]))
            put_state(outs[m], e, *total)


def prepare_kernel(group_size, q_ref, k_ref, v_ref, halo_ref, _, q_wide, kx, vt):
    rows, _, width = q_ref.shape
    for g in range(k_ref.shape[0]):
        q = q_ref[:, g * group_size : (g + 1) * group_size].astype(F32)
        q_wide[g] = q.reshape(rows * group_size, width)
        kx[g, :WINDOW] = halo_ref[0, g]
        kx[g, WINDOW:] = k_ref[g]
        vt[g] = jnp.concatenate([halo_ref[1, g], v_ref[g]], axis=0).T


def near_kernel(group_size, per_part, first, count, idx_ref, share_ref, q_wide, kx_ref, vt_ref, feat_ref, wq_ref, wk_ref, *refs):
    num_ref, den_ref, qf_ref, fx = refs[-4:]
    out = pl.program_id(0) * count
    slot = first + out
    head = lax.bitwise_xor(idx_ref[0], slot // per_part) * per_part + slot % per_part
    g = head // group_size
    rows, width = feat_ref.shape[1:]
    scale = np.float32(np.log2(np.e) / np.sqrt(width))
    kx, vt = kx_ref.at[g], vt_ref.at[g]
    present = idx_ref[1] > 0
    block = 128
    span = block + WINDOW
    key = lax.broadcasted_iota(jnp.int32, (span, 2 * block), 0)
    row = lax.broadcasted_iota(jnp.int32, (span, 2 * block), 1) % block
    band = (key > row) & (key <= row + WINDOW)
    wide = 2 * block
    causal = lax.broadcasted_iota(jnp.int32, (wide, wide), 0) <= lax.broadcasted_iota(jnp.int32, (wide, wide), 1)
    halo_logits = mm(wk_ref[pl.ds(head, count)].reshape(-1, width), kx[:128], 1, 1)
    feat = halo_logits.shape[0] // count
    for pair in range(0, count, 2):
        qs, mixes, rests, lnums, lsums = [], [], [], [], []
        products, logits = [], [[], []]
        for r in range(rows // block):
            at = r * block
            both = jnp.concatenate(
                [
                    q_wide[g, pl.ds(at * group_size + head % group_size + e, block, stride=group_size), :].astype(BF)
                    for e in (pair, pair + 1)
                ],
                axis=0,
            )
            maps = [wq_ref[head + pair], wq_ref[head + pair + 1], kx[at : at + span]]
            x = mm(jnp.concatenate(maps, axis=0), both, 1, 1)
            logits[0].append(x[:feat, :block])
            logits[1].append(x[feat : 2 * feat, block:])
            products.append(x[2 * feat :])
        for e in (pair, pair + 1):
            halo_feat = features_t(halo_logits[e * feat : (e + 1) * feat]).T[:WINDOW]
            fx[e, :WINDOW] = jnp.where(present, halo_feat.astype(F32), 0.0).astype(BF)
            fx[e, WINDOW:] = feat_ref[head + e]
            mixes.append(jax.nn.sigmoid(jnp.full((1, block), share_ref[head + e], F32)))
            rests.append(1.0 - mixes[-1])
            qf = features_t(jnp.concatenate(logits[e - pair], axis=1))
            qf_ref[out + e] = qf
            for r in range(rows // wide):
                at = r * wide
                lnum = None
                lsum = None
                for kc in range(r + 1):
                    a = mm(fx[e, kc * wide : kc * wide + wide], qf[:, at : at + wide])
                    if kc == r:
                        last = jnp.where(causal, a, 0.0)
                    else:
                        last = a
                    if kc == 0:
                        halo = a[:WINDOW]
                        kept = halo.astype(BF).astype(F32)
                        body = last[WINDOW:]
                        part = jnp.sum(body, axis=0, keepdims=True)
                        if r == 0:
                            inside = causal[:WINDOW]
                            kept = jnp.where(inside, kept, 0.0)
                            part = part - jnp.sum(jnp.where(inside, 0.0, halo), axis=0, keepdims=True)
                        w = jnp.concatenate([(kept - halo).astype(BF), body.astype(BF)], axis=0)
                    else:
                        w = last.astype(BF)
                        part = jnp.sum(last, axis=0, keepdims=True)
                    t = mm(vt[:, kc * wide : kc * wide + wide], w)
                    lnum = t if lnum is None else lnum + t
                    lsum = part if lsum is None else lsum + part
                lnums.append(lnum)
                lsums.append(lsum)
        for r in range(rows // block):
            at = r * block
            mask = (band & ((key >= WINDOW) | present)) if r == 0 else band
            s = jnp.where(mask, products[r], -1e30)
            p = jnp.exp2((s - jnp.max(s, axis=0, keepdims=True)) * scale)
            wsum = jnp.sum(p, axis=0, keepdims=True)
            wnum = mm(vt[:, at : at + span], p.astype(BF))
            for k in range(2):
                mine = slice(k * block, (k + 1) * block)
                mixed = k * (rows // wide) + at // wide
                part = slice(at % wide, at % wide + block)
                num_ref[out + pair + k, :, at : at + block] = (
                    mixes[k] * wnum[:, mine] + rests[k] * lnums[mixed][:, part]
                )
                den_ref[out + pair + k, :, at : at + block] = (
                    mixes[k] * wsum[:, mine] + rests[k] * lsums[mixed][:, part]
                )


def finished(per_part, which, half, first, idx_ref, share_ref, held, pieces):
    at = pl.ds(pl.multiple_of(idx_ref[which] * half, 128), half)
    slot = 0
    for num, den, qf in held:
        count, width, _ = num.shape
        for n in range(count):
            m, e = divmod(slot, per_part)
            slot += 1
            if not first <= m < first + len(pieces):
                continue
            head = lax.bitwise_xor(idx_ref[0], m) * per_part + e
            rest = 1.0 - jax.nn.sigmoid(jnp.full((1, half), share_ref[head], F32))
            both = mm(pieces[m - first][e], qf[n, :, at])
            numer = num[n, :, at] + rest * both[:width]
            denom = den[n, :, at] + rest * (both[width : width + 1] + both[width + 1 : width + 2])
            yield m, e, (numer * (1.0 / denom)).astype(BF).T


def quarter_at(core, m, per_part, idx_ref):
    return pl.ds((idx_ref[core] * PART + lax.bitwise_xor(idx_ref[0], m)) * per_part, per_part)


def final_own_kernel(per_part, half, idx_ref, share_ref, num, den, qf, piece, sent_ref, kept):
    held, pieces = [(num, den, qf)], [piece]
    for _, e, rows in finished(per_part, 3, half, 0, idx_ref, share_ref, held, pieces):
        sent_ref[e] = rows
    for _, e, rows in finished(per_part, 2, half, 0, idx_ref, share_ref, held, pieces):
        kept[e] = rows


def final_sent_kernel(per_part, half, idx_ref, share_ref, *refs):
    held, pieces, out_ref = [refs[k : k + 3] for k in range(0, 9, 3)], refs[9 : 8 + PART], refs[-1]
    for m, e, rows in finished(per_part, 3, half, 1, idx_ref, share_ref, held, pieces):
        out_ref[(m - 1) * per_part + e] = rows


def final_kept_kernel(per_part, half, idx_ref, share_ref, *refs):
    held, pieces, kept_own = [refs[k : k + 3] for k in range(0, 9, 3)], refs[9 : 8 + PART], refs[8 + PART]
    out_ref, kept, sems = refs[-3:]
    copies = [pltpu.make_async_copy(kept_own, out_ref.at[quarter_at(2, 0, per_part, idx_ref)], sems.at[0])]
    copies[0].start()
    for m, e, rows in finished(per_part, 2, half, 1, idx_ref, share_ref, held, pieces):
        kept[m - 1, e] = rows
        if e == per_part - 1:
            copies.append(
                pltpu.make_async_copy(kept.at[m - 1], out_ref.at[quarter_at(2, m, per_part, idx_ref)], sems.at[m])
            )
            copies[-1].start()
    for copy in copies:
        copy.wait()


def place_kernel(per_part, idx_ref, own_ref, got_ref, _, out_ref, sems):
    copies = [
        pltpu.make_async_copy(
            got_ref.at[pl.ds((m - 1) * per_part, per_part)] if m else own_ref,
            out_ref.at[quarter_at(3, m, per_part, idx_ref)],
            sems.at[m],
        )
        for m in range(PART)
    ]
    for copy in copies:
        copy.start()
    for copy in copies:
        copy.wait()


def per_device(queries, key_vectors, value_vectors, query_map, key_map, window_param):
    rows, heads, width = queries.shape
    groups = key_vectors.shape[1]
    group_size = heads // groups
    feat = query_map.shape[2]
    per_part = heads // PART
    tall = width + 8
    devices = lax.axis_size("seq")
    zs = devices // PART
    position = lax.axis_index("seq")
    core = lax.axis_index("head")
    me = position % PART
    idx = jnp.stack([me, position, core, 1 - core]).astype(jnp.int32)
    params = pltpu.CompilerParams(vmem_limit_bytes=LIMIT)
    smem = pl.BlockSpec(memory_space=pltpu.SMEM)
    anywhere = pl.BlockSpec(memory_space=pl.ANY)
    vmem = pl.BlockSpec(memory_space=pltpu.VMEM)
    query_map = query_map.transpose(0, 2, 1)
    key_map = key_map.transpose(0, 2, 1)

    def xor(x, m):
        return lax.ppermute(x, "seq", [(i, i ^ m) for i in range(devices)])

    def shift(x, by):
        return lax.ppermute(x, "seq", [(i, i + by) for i in range(devices - by)])

    piece_shape = jax.ShapeDtypeStruct((per_part, tall, width), BF)
    grouped = jax.ShapeDtypeStruct((groups, rows, width), BF)
    feat_shape = jax.ShapeDtypeStruct((heads, rows, width), BF)
    hbm = pl.BlockSpec(memory_space=pltpu.HBM)
    own_feat, keys, values, values_t, key_map, *pieces = pl.pallas_call(
        functools.partial(sent_states_kernel, per_part, group_size),
        in_specs=[smem] + [hbm] * 3,
        out_specs=[vmem] * (5 + PART - 1),
        out_shape=[
            feat_shape,
            grouped,
            grouped,
            jax.ShapeDtypeStruct((groups, tall, rows), BF),
            jax.ShapeDtypeStruct(key_map.shape, BF),
        ]
        + [piece_shape] * (PART - 1),
        scratch_shapes=[
            pltpu.VMEM((rows, groups, width), BF),
            pltpu.VMEM((rows, groups, width), BF),
            pltpu.SemaphoreType.DMA((6,)),
        ],
        compiler_params=params,
        name="sent_states",
    )(idx, *(pltpu.with_memory_space_constraint(x, pltpu.HBM) for x in (key_vectors, value_vectors, key_map)))
    pieces = [xor(pieces[m - 1], m) for m in range(1, PART)]
    own_feat, own_piece, tails = pl.pallas_call(
        functools.partial(own_states_kernel, per_part, group_size),
        in_specs=[smem] + [vmem] * 5,
        out_specs=[vmem] * 3,
        out_shape=[feat_shape, piece_shape, jax.ShapeDtypeStruct((2, groups, WINDOW, width), BF)],
        input_output_aliases={5: 0},
        compiler_params=params,
        cost_estimate=pl.CostEstimate(flops=10**9, bytes_accessed=2 * 10**6, transcendentals=10**6),
        name="own_states",
    )(idx, keys, values, values_t, key_map, own_feat)
    halo = shift(tails, 1)
    pieces = [own_piece] + pieces
    total = pl.pallas_call(
        total_kernel, in_specs=[vmem] * PART, out_specs=vmem, out_shape=piece_shape, compiler_params=params, name="totals"
    )(*pieces)
    exchanged = zs in (1, 2, 4)
    if exchanged:
        earlier = [xor(total, PART * k) for k in range(1, min(zs, 2))]
    else:
        columns = [[z * PART + k for z in range(zs)] for k in range(PART)]
        gathered = lax.all_gather(total, "seq", axis_index_groups=columns)
        below = jnp.arange(zs) < position // PART
        summed = jnp.sum(jnp.where(below[:, None, None, None], gathered.astype(F32), 0.0), axis=0)
        high = summed.astype(BF)
        earlier = [high, (summed - high.astype(F32)).astype(BF)]
    q_wide, keys, values = pl.pallas_call(
        functools.partial(prepare_kernel, group_size),
        in_specs=[vmem] * 4 + [anywhere],
        out_specs=[vmem] * 3,
        out_shape=[
            jax.ShapeDtypeStruct((groups, rows * group_size, width), F32),
            jax.ShapeDtypeStruct((groups, WINDOW + rows, width), BF),
            jax.ShapeDtypeStruct((groups, width, WINDOW + rows), BF),
        ],
        compiler_params=params,
        name="prepare",
    )(queries, keys, values, halo, total)

    def near(first, count, after):
        return pl.pallas_call(
            functools.partial(near_kernel, group_size, per_part, first, STEP),
            grid=(count // STEP,),
            in_specs=[smem, smem] + [vmem] * 6 + [anywhere] * len(after),
            out_specs=[vmem] * 3,
            scratch_shapes=[pltpu.VMEM((STEP, WINDOW + rows, 2 * feat), BF)],
            out_shape=[
                jax.ShapeDtypeStruct((count, width, rows), F32),
                jax.ShapeDtypeStruct((count, 1, rows), F32),
                jax.ShapeDtypeStruct((count, 2 * feat, rows), BF),
            ],
            compiler_params=params,
            cost_estimate=pl.CostEstimate(
                flops=count * 4 * 10**8, bytes_accessed=count * 10**6, transcendentals=count * 3 * 10**5
            ),
            name="near_%d" % first,
        )(idx, window_param, q_wide, keys, values, own_feat, query_map, key_map, *after)

    held = list(near(0, SPLIT[0], []))
    if zs == 4:
        pair = pl.pallas_call(
            sum_kernel,
            in_specs=[vmem] * 2 + [anywhere],
            out_specs=vmem,
            out_shape=piece_shape,
            compiler_params=params,
            name="layer_sum",
        )(total, earlier[0], held[1])
        earlier.append(xor(pair, 2 * PART))
        held += near(SPLIT[0], SPLIT[1] - SPLIT[0], [pair])
    else:
        held += near(SPLIT[0], SPLIT[1] - SPLIT[0], [])
    prefixes = pl.pallas_call(
        functools.partial(prefix_kernel, len(earlier), exchanged),
        in_specs=[smem] + [vmem] * (PART + len(earlier)) + [anywhere],
        out_specs=[vmem] * PART,
        out_shape=[piece_shape] * PART,
        compiler_params=params,
        name="prefixes",
    )(idx, *pieces, *earlier, held[4])
    prior = [prefixes[0]] + [xor(prefixes[m], m) for m in range(1, PART)]
    held += near(SPLIT[1], heads - SPLIT[1], [prefixes[0]])

    half = rows // 2
    out_shape = jax.ShapeDtypeStruct((2 * heads, half, width), BF)

    def swapped(x):
        return lax.ppermute(x, "head", [(0, 1), (1, 0)])

    sent_own, kept_own = pl.pallas_call(
        functools.partial(final_own_kernel, per_part, half),
        in_specs=[smem, smem] + [vmem] * 4,
        out_specs=[vmem] * 2,
        out_shape=[jax.ShapeDtypeStruct((per_part, half, width), BF)] * 2,
        compiler_params=params,
        cost_estimate=pl.CostEstimate(flops=5 * 10**8, bytes_accessed=2 * 10**6, transcendentals=0),
        name="final_own",
    )(idx, window_param, *held[:3], prior[0])
    got_own = swapped(sent_own)
    sent = pl.pallas_call(
        functools.partial(final_sent_kernel, per_part, half),
        in_specs=[smem, smem] + [vmem] * (8 + PART) + [anywhere],
        out_specs=vmem,
        out_shape=jax.ShapeDtypeStruct((heads - per_part, half, width), BF),
        compiler_params=params,
        name="final_sent",
    )(idx, window_param, *held, *prior[1:], sent_own)
    got = swapped(sent)
    out = pl.pallas_call(
        functools.partial(final_kept_kernel, per_part, half),
        in_specs=[smem, smem] + [vmem] * (9 + PART) + [anywhere],
        out_specs=hbm,
        out_shape=out_shape,
        scratch_shapes=[pltpu.VMEM((PART - 1, per_part, half, width), BF), pltpu.SemaphoreType.DMA((PART,))],
        compiler_params=params,
        cost_estimate=pl.CostEstimate(flops=10**9, bytes_accessed=5 * 10**6, transcendentals=0),
        name="final_kept",
    )(idx, window_param, *held, *prior[1:], kept_own, sent)
    return pl.pallas_call(
        functools.partial(place_kernel, per_part),
        in_specs=[smem, vmem, vmem, hbm],
        out_specs=hbm,
        out_shape=out_shape,
        scratch_shapes=[pltpu.SemaphoreType.DMA((PART,))],
        input_output_aliases={3: 0},
        compiler_params=params,
        name="place",
    )(idx, got_own, got, out)


def solution(mesh):
    in_specs = (
        P("seq", "head", None),
        P("seq", "head", None),
        P("seq", "head", None),
        P("head", None, None),
        P("head", None, None),
        P("head"),
    )
    out_specs = P(None, ("seq", "head"), None)
    return jax.shard_map(
        per_device, mesh=mesh, in_specs=in_specs, out_specs=out_specs, check_vma=False
    )
```
